512 devices in a mesh: fsdp: 64 (over z_lo, x, core), tp: 8 (over z_hi, y).
Axes of the slice: x: 4, y: 4, z: 16 (z_hi: 2, z_lo: 8; z = z_hi * 8 + z_lo), core: 2. Of those that a mesh axis runs over, the one named last changes fastest.
Arguments:
- train_inputs: bfloat16 [65536, 8192], P('fsdp', 'tp'), may hold values from -6 to 6
- key_cotangent: bfloat16 [65536, 1024], P('fsdp'), may hold values from -0.0234375 to 0.0234375
- master: float32 [8, 1024, 1024], P('tp', 'fsdp'), may hold values from -0.125 to 0.125
- moment_one: float32 [8, 1024, 1024], P('tp', 'fsdp'), may hold values from -6 to 6
- moment_two: float32 [8, 1024, 1024], P('tp', 'fsdp'), may hold values from 0.25 to 4
- step_inputs: bfloat16 [3, 256, 8192], P(None, 'fsdp', 'tp'), may hold values from -6 to 6
- decode_queries: bfloat16 [3, 256, 64, 128], P(None, 'fsdp', 'tp'), may hold values from -8 to 8
- step_values: bfloat16 [3, 256, 8, 128], P(None, 'fsdp', 'tp'), may hold values from -6 to 6
- cache_keys: bfloat16 [256, 8, 512, 128], P('fsdp', 'tp'), may hold values from -6 to 6
- cache_values: bfloat16 [256, 8, 512, 128], P('fsdp', 'tp'), may hold values from -6 to 6
- cache_lengths: int32 [256], P('fsdp'), may hold values from 128 to 512, as said below
- norm_gain: float32 [8192], replicated, may hold values from 0.1 to 1.9
Outputs:
- new_master: float32 [8, 1024, 1024], P('tp', 'fsdp')
- new_moment_one: float32 [8, 1024, 1024], P('tp', 'fsdp')
- new_moment_two: float32 [8, 1024, 1024], P('tp', 'fsdp')
- new_keys: bfloat16 [3, 256, 8, 128], P(None, 'fsdp', 'tp')
- decoded: bfloat16 [3, 256, 8192], P(None, 'fsdp', 'tp')
The draws below stay inside these ranges and needn't reach their ends.
Inputs may be any that keep to these rules, and one draw needn't show every extreme that they name: `cache_lengths`: some row has exactly 512 live slots in every draw.
All inputs are finite; a program needn't handle non-finite values.
Results may differ from the reference program's by a relative error of at most 0.0055.
The reference program's roundings to bfloat16 on the way count: a program that leaves them out, or rounds other values in their place, can miss the bound.
Values may be sent and summed in bfloat16 or wider, within the bound.
A program may use at most 64 MiB of HBM per device.

```python
import math
import jax
import jax.numpy as jnp
from jax import lax

D = 8192
HEADS = 64
KVH = 8
HD = 128
DSTEPS = 3
CACHE = 512
TOKENS = 65536
ROWS = 256
N_TP = 8


def draw_decode_queries(key, part):
    own_key = jax.random.fold_in(key, 11)
    shape = (DSTEPS, ROWS, HEADS, HD)
    return jnp.clip(2.0 * jax.random.normal(own_key, shape, jnp.float32), -8.0, 8.0).astype(jnp.bfloat16)


def draw_cache_keys(key, part):
    own_key = jax.random.fold_in(key, 7)
    shape = (ROWS, KVH, CACHE, HD)
    return jnp.clip(jax.random.normal(own_key, shape, jnp.float32), -6.0, 6.0).astype(jnp.bfloat16)


def draw_cache_lengths(key, part):
    key = jax.random.fold_in(key, 5)
    first_key, second_key = jax.random.split(key)
    lengths = jax.random.randint(first_key, (ROWS,), CACHE // 4, CACHE + 1)
    picked = jax.random.randint(second_key, (), 0, ROWS)
    return jnp.where(jnp.arange(ROWS) == picked, CACHE, lengths).astype(jnp.int32)


def block_scale(key, dims, shards, low, top_value):
    loudness, own = 1.0, jax.random.fold_in(key, 6)
    for dim, shards_of in shards:
        heights = jnp.exp(jax.random.uniform(jax.random.fold_in(own, dim), (shards_of,), jnp.float32, low / len(shards), top_value / len(shards)))
        loudness = loudness * jnp.repeat(heights, dims[dim] // shards_of).reshape([-1 if axis == dim else 1 for axis in range(len(dims))])
    return loudness


def scatter_about(rng, dims, width, limit, cuts=(), held_as=jnp.bfloat16):
    level = block_scale(rng, dims, cuts, -0.22, 0.18) if cuts else 1.0
    array = jax.random.normal(rng, dims, jnp.float32) * width * level
    return jnp.minimum(jnp.maximum(array, -limit), limit).astype(held_as)


def setup_inputs(seed: int = 0) -> dict:
    streams_of = jax.random.split(jax.random.key(seed), 13)
    train_inputs = scatter_about(streams_of[0], (TOKENS, D), 1.0, 6.0, ((0, 64), (1, 8)))
    key_cotangent = scatter_about(streams_of[1], (TOKENS, KVH * HD), TOKENS ** -0.5, 0.0234375, ((0, 64),))
    master = scatter_about(streams_of[2], (N_TP, D // N_TP, KVH * HD), (D // 4) ** -0.5, 0.125, ((0, 8), (1, 64)), jnp.float32)
    moment_one = scatter_about(streams_of[3], (N_TP, D // N_TP, KVH * HD), 1.0, 6.0, ((0, 8), (1, 64)), jnp.float32)
    moment_two = jnp.clip(jnp.exp(math.log(4.0) - 2.7725887 * jax.random.uniform(streams_of[4], (N_TP, D // N_TP, KVH * HD), jnp.float32) ** block_scale(streams_of[4], (N_TP, D // N_TP, KVH * HD), ((0, 8), (1, 64)), -0.2, 0.2)), 0.25, 4.0)
    step_inputs = scatter_about(streams_of[5], (DSTEPS, ROWS, D), 1.0, 6.0, ((1, 64), (2, 8)))
    decode_queries = draw_decode_queries(jax.random.fold_in(streams_of[12], 71), 0)
    step_values = scatter_about(streams_of[7], (DSTEPS, ROWS, KVH, HD), 1.0, 6.0, ((1, 64), (2, 8)))
    cache_keys = draw_cache_keys(jax.random.fold_in(streams_of[12], 71), 0)
    cache_values = scatter_about(streams_of[9], (ROWS, KVH, CACHE, HD), 1.0, 6.0, ((0, 64), (1, 8)))
    cache_lengths = draw_cache_lengths(jax.random.fold_in(streams_of[12], 71), 0)
    norm_gain = jnp.clip(1.0 + 0.18 * jax.random.normal(streams_of[11], (D,), jnp.float32), 0.1, 1.9)
    return dict(train_inputs=train_inputs, key_cotangent=key_cotangent, master=master, moment_one=moment_one, moment_two=moment_two, step_inputs=step_inputs, decode_queries=decode_queries, step_values=step_values, cache_keys=cache_keys, cache_values=cache_values, cache_lengths=cache_lengths, norm_gain=norm_gain)


correction_one = 1.0 - 0.9 ** 4
correction_two = 1.0 - 0.95 ** 4

def attend_row(row):
    queries, keys_new, values_new, keys_old, values_old, length = row
    group = HEADS // KVH
    queries = queries.astype(jnp.float32).reshape(DSTEPS, KVH, group, HD)
    keys_old = keys_old.astype(jnp.float32)
    values_old = values_old.astype(jnp.float32)
    keys_new = keys_new.astype(jnp.float32)
    values_new = values_new.astype(jnp.float32)
    scale = 1.0 / HD ** 0.5
    old_scores = jnp.einsum('skgd,kpd->skgp', queries, keys_old) * scale
    slots = jnp.arange(CACHE, dtype=jnp.int32)
    old_scores = jnp.where((slots < length)[None, None, None, :], old_scores, -jnp.inf)
    new_scores = jnp.einsum('skgd,jkd->skgj', queries, keys_new) * scale
    causal = jnp.arange(DSTEPS)[None, :] <= jnp.arange(DSTEPS)[:, None]
    new_scores = jnp.where(causal[:, None, None, :], new_scores, -jnp.inf)
    top = jnp.maximum(lax.optimization_barrier(jnp.max(old_scores, axis=-1)), lax.optimization_barrier(jnp.max(new_scores, axis=-1)))[..., None]
    old_weights = jnp.exp(old_scores - top)
    new_weights = jnp.exp(new_scores - top)
    total = lax.optimization_barrier(jnp.sum(old_weights, axis=-1, keepdims=True)) + lax.optimization_barrier(jnp.sum(new_weights, axis=-1, keepdims=True))
    old_probs = (old_weights / total).astype(jnp.bfloat16).astype(jnp.float32)
    new_probs = (new_weights / total).astype(jnp.bfloat16).astype(jnp.float32)
    attended = jnp.einsum('skgp,kpd->skgd', old_probs, values_old) + jnp.einsum('skgj,jkd->skgd', new_probs, values_new)
    return attended.reshape(DSTEPS, D)

def reference(train_inputs, key_cotangent, master, moment_one, moment_two, step_inputs, decode_queries, step_values, cache_keys, cache_values, cache_lengths, norm_gain):
    gradient = jnp.dot(train_inputs.T, key_cotangent, preferred_element_type=jnp.float32).reshape(master.shape)
    new_moment_one = 0.9 * moment_one + 0.1 * gradient
    new_moment_two = 0.95 * moment_two + 0.05 * gradient * gradient
    new_master = master - 0.003 * (new_moment_one / correction_one) / (jnp.sqrt(new_moment_two / correction_two) + 1e-08)
    weights = new_master.reshape(D, KVH * HD).astype(jnp.bfloat16)
    inputs_flat = step_inputs.astype(jnp.float32).reshape(DSTEPS * ROWS, D)
    inverse = lax.rsqrt(lax.optimization_barrier(jnp.mean(inputs_flat * inputs_flat, axis=-1, keepdims=True)) + 1e-06)
    normed = (inputs_flat * inverse * norm_gain).astype(jnp.bfloat16)
    new_keys = jnp.dot(normed, weights, preferred_element_type=jnp.float32).astype(jnp.bfloat16).reshape(DSTEPS, ROWS, KVH, HD)
    rows_first = (jnp.swapaxes(decode_queries, 0, 1), jnp.swapaxes(new_keys, 0, 1), jnp.swapaxes(step_values, 0, 1), cache_keys, cache_values, cache_lengths)
    attended = jnp.swapaxes(lax.map(attend_row, rows_first), 0, 1)
    decoded = (step_inputs.astype(jnp.float32) + attended).astype(jnp.bfloat16)
    return (new_master, new_moment_one, new_moment_two, new_keys, decoded)
```

```python
import functools

import jax
import jax.numpy as jnp
from jax import lax
from jax.experimental import pallas as pl
from jax.experimental.pallas import tpu as pltpu
from jax.sharding import PartitionSpec as P

MESH = pl.DeviceIdType.MESH
correction_one = 1.0 - 0.9**4
correction_two = 1.0 - 0.95**4

CHUNKS = 4
CW = 1024 // CHUNKS
F32 = jnp.float32
BF16 = jnp.bfloat16


class Copies:
    def __init__(self, send_sems, recv_sems):
        self.send_sems, self.recv_sems = send_sems, recv_sems
        self.made = []

    def send(self, src, dst, device):
        number = len(self.made)
        copy = pltpu.make_async_remote_copy(
            src_ref=src,
            dst_ref=dst,
            send_sem=self.send_sems.at[number],
            recv_sem=self.recv_sems.at[number],
            device_id=device,
            device_id_type=MESH,
        )
        copy.start()
        self.made.append(copy)
        return copy


N_COPIES = 25 + 11 * CHUNKS + 25


def kernel(
    x_hbm,
    c_hbm,
    master_hbm,
    one_hbm,
    two_hbm,
    step_hbm,
    query_hbm,
    value_hbm,
    ck_hbm,
    cv_hbm,
    lengths,
    gain_hbm,
    new_master,
    new_one,
    new_two,
    keys_out,
    att_out,
    x_v,
    c_v,
    adam_v,
    step_v,
    query_v,
    value_v,
    ck_v,
    cv_v,
    gain_v,
    part,
    part_in,
    ring_out,
    ring_in,
    line_sum,
    pair_out,
    pair_in,
    quad_sum,
    quad_out,
    quad_in,
    rows32,
    rows_y,
    rows_z,
    squares,
    normed,
    w_out,
    w_all,
    key_part,
    key_in,
    q32,
    old_exp,
    old_top,
    old_sum,
    sv32,
    local_sems,
    send_sems,
    recv_sems,
):
    f, t = lax.axis_index("fsdp"), lax.axis_index("tp")
    core = lax.rem(f, 2)
    x = lax.rem(lax.div(f, 2), 4)
    zl = lax.div(f, 8)
    y = lax.rem(t, 4)
    zh = lax.div(t, 4)
    z = zh * 8 + zl

    def fsdp(zl_, x_, core_):
        return (zl_ * 4 + x_) * 2 + core_

    def at(zl_=zl, x_=x, core_=core, zh_=zh, y_=y):
        return {"fsdp": fsdp(zl_, x_, core_), "tp": zh_ * 4 + y_}

    sibling = at(core_=1 - core)
    x_peer = [None] + [at(x_=lax.rem(x + k, 4)) for k in (1, 2, 3)]
    y_peer = [None] + [at(y_=lax.rem(y + k, 4)) for k in (1, 2, 3)]

    def z_of(k):
        return lax.rem(z + k, 16)

    def z_peer(k):
        other = z_of(k)
        return at(zl_=lax.rem(other, 8), zh_=lax.div(other, 8))

    barrier = pltpu.get_barrier_semaphore()
    partners = [sibling] + x_peer[1:] + y_peer[1:] + [z_peer(k) for k in range(1, 16)]
    for partner in partners:
        pl.semaphore_signal(barrier, inc=1, device_id=partner, device_id_type=MESH)

    loads = []
    for number, (src, dst) in enumerate(
        (
            (x_hbm, x_v),
            (c_hbm, c_v),
            (step_hbm, step_v),
            (query_hbm, query_v),
            (ck_hbm, ck_v),
            (cv_hbm, cv_v),
            (value_hbm, value_v),
            (gain_hbm, gain_v),
            (master_hbm, adam_v.at[0]),
            (one_hbm, adam_v.at[1]),
            (two_hbm, adam_v.at[2]),
        )
    ):
        load = pltpu.make_async_copy(src, dst, local_sems.at[number])
        load.start()
        loads.append(load)

    loads[2].wait()
    rows32[...] = jnp.zeros_like(rows32)
    for s in range(3):
        rows32[4 * s : 4 * s + 4, :] = step_v[s].astype(F32)
    for k in range(8):
        rows_y[y, k] = rows32[:, 128 * k : 128 * k + 128].astype(BF16)

    loads[0].wait()
    loads[1].wait()
    for j in range(CHUNKS):

        @pl.loop(0, 8)
        def _(m):
            columns = pl.ds(pl.multiple_of(m * 128, 128), 128)
            term = lax.dot_general(
                x_v[:, columns],
                c_v[:, j * CW : (j + 1) * CW],
                (((0,), (0,)), ((), ())),
                preferred_element_type=F32,
            ).reshape(4, 2, 16, CW)
            part[j, 0, m] = term[:, 0]
            part[j, 1, m] = term[:, 1]

    pl.semaphore_wait(barrier, len(partners))
    copies = Copies(send_sems, recv_sems)

    own_rows = [copies.send(rows_y.at[y], rows_y.at[y], y_peer[k]) for k in (1, 2, 3)]
    swaps = [
        copies.send(part.at[j, 1 - core], part_in.at[j], sibling) for j in range(CHUNKS)
    ]

    xp, xo, xm = (lax.rem(x + k, 4) for k in (1, 2, 3))
    low, high = slice(0, 4), slice(4, 8)
    ring, pairs, quads = {}, {}, {}
    parity, quad = lax.rem(zl, 2), lax.div(zl, 2)

    def chip_sum(j, half, target):
        return part[j, core, half, target] + part_in[j, half, target]

    def ring_send(j, number, value, device):
        ring_out[j, number] = value.astype(BF16)
        ring[j, number] = copies.send(ring_out.at[j, number], ring_in.at[j, number], device)

    def ring_first(j):
        swaps[j].wait_recv()
        ring_send(j, 0, chip_sum(j, low, xo), x_peer[1])
        ring_send(j, 1, chip_sum(j, high, xo), x_peer[3])
        ring_send(j, 2, chip_sum(j, high, xp), x_peer[1])
        ring_send(j, 3, chip_sum(j, low, xm), x_peer[3])

    def ring_second(j):
        ring[j, 0].wait_recv()
        ring_send(j, 4, chip_sum(j, low, xp) + ring_in[j, 0].astype(F32), x_peer[1])
        ring[j, 1].wait_recv()
        ring_send(j, 5, chip_sum(j, high, xm) + ring_in[j, 1].astype(F32), x_peer[3])

    def line_pair(j):
        for number in (2, 3, 4, 5):
            ring[j, number].wait_recv()
        line_sum[j, low] = (
            chip_sum(j, low, x) + ring_in[j, 3].astype(F32) + ring_in[j, 4].astype(F32)
        )
        line_sum[j, high] = (
            chip_sum(j, high, x) + ring_in[j, 2].astype(F32) + ring_in[j, 5].astype(F32)
        )
        for q in range(4):
            pair_out[j, q] = line_sum[j, 2 * q + 1 - parity].astype(BF16)
        pairs[j] = copies.send(
            pair_out.at[j], pair_in.at[j], at(zl_=zl + 1 - 2 * parity)
        )

    def line_quad(j):
        pairs[j].wait_recv()
        for q in range(4):
            total = line_sum[j, 2 * q + parity] + pair_in[j, q].astype(F32)
            quad_sum[j, q] = total
            quad_out[j, q] = total.astype(BF16)
        for k in (2, 3, 1):
            other = lax.rem(quad + k, 4)
            quads[j, k] = copies.send(
                quad_out.at[j, other], quad_in.at[j, k - 1], at(zl_=2 * other + parity)
            )

    def update(j):
        for k in (1, 2, 3):
            quads[j, k].wait_recv()
        gradient = quad_sum[j, quad]
        for k in (1, 2, 3):
            gradient = gradient + quad_in[j, k - 1].astype(F32)
        columns = slice(j * CW, (j + 1) * CW)
        one = 0.9 * adam_v[1, 0, :, columns] + 0.1 * gradient
        two = 0.95 * adam_v[2, 0, :, columns] + 0.05 * gradient * gradient
        fresh = adam_v[0, 0, :, columns] - 0.003 * (one / correction_one) / (
            jnp.sqrt(two / correction_two) + 1e-08
        )
        new_one[0, :, columns] = one
        new_two[0, :, columns] = two
        new_master[0, :, columns] = fresh
        weights = fresh.astype(BF16)
        for k in range(CW // 128):
            head = j * (CW // 128) + k
            w_out[head % 4, head // 4] = weights[:, 128 * k : 128 * k + 128]

    lane = lax.broadcasted_iota(jnp.int32, (16, 128), 1)
    diagonal = lane == lax.broadcasted_iota(jnp.int32, (16, 128), 0)
    spread, rows_sent = {}, {}

    def send_rows():
        for copy in own_rows:
            copy.wait_recv()
        for k in (4, 3, 5, 2, 6, 1, 7):
            other = lax.rem(zl + k, 8)
            rows_sent[k] = copies.send(rows_y.at[:, other], rows_z.at[zl], at(zl_=other))
        total = jnp.zeros((16, 128), F32)
        for q in range(4):
            for k in range(8):
                block = rows_y[q, k].astype(F32)
                total = total + block * block
        column = jnp.sum(total, axis=1, keepdims=True)
        squares[z] = jnp.sum(jnp.where(diagonal, column, 0.0), axis=0, keepdims=True)
        for k in (8, 7, 9, 6, 10, 5, 11, 4, 12, 3, 13, 2, 14, 1, 15):
            spread[k] = copies.send(squares.at[z], squares.at[z], z_peer(k))
        for q in range(4):
            rows_z[zl, q] = rows_y[q, zl]

    def make_normed():
        for k in range(1, 16):
            spread[k].wait_recv()
        for k in range(1, 8):
            rows_sent[k].wait_recv()
        for s in range(8):
            both = squares[s] + squares[s + 8]
            column = jnp.sum(jnp.where(diagonal, both, 0.0), axis=1, keepdims=True)
            inverse = lax.rsqrt(column * (1.0 / 8192.0) + 1e-06)
            for q in range(4):
                gain = gain_v[pl.ds((zh * 4 + q) * 8 + zl, 1), :]
                block = rows_z[s, q].astype(F32) * inverse * gain
                normed[16 * s : 16 * s + 16, 128 * q : 128 * q + 128] = block.astype(BF16)

    scale = 1.0 / 128.0**0.5

    def old_scores():
        for number in (3, 4, 5, 6):
            loads[number].wait()
        q32[...] = jnp.zeros_like(q32)
        for s in range(3):
            for r in range(4):
                q32[32 * r + 8 * s : 32 * r + 8 * s + 8, :] = query_v[s, r].astype(F32)
        sv32[...] = jnp.zeros_like(sv32)
        for s in range(3):
            sv32[4 * s : 4 * s + 4, :] = value_v[s, :, 0, :].astype(F32)
        slot = lax.broadcasted_iota(jnp.int32, (32, 512), 1)
        for r in range(4):
            scores = (
                lax.dot_general(
                    q32[32 * r : 32 * r + 32, :].astype(BF16),
                    ck_v[r, 0],
                    (((1,), (1,)), ((), ())),
                    preferred_element_type=F32,
                )
                * scale
            )
            scores = jnp.where(slot < lengths[r], scores, -jnp.inf)
            top = jnp.max(scores, axis=1, keepdims=True)
            weight = jnp.exp(scores - top)
            rows = slice(32 * r, 32 * r + 32)
            old_exp[rows, :] = weight
            old_top[rows, :] = top
            old_sum[rows, :] = jnp.sum(weight, axis=1, keepdims=True)

    ring_first(0)
    send_rows()
    ring_first(1)
    ring_second(0)
    line_pair(0)
    ring_first(2)
    ring_second(1)
    old_scores()
    line_quad(0)
    line_pair(1)
    ring_first(3)
    ring_second(2)
    line_quad(1)
    line_pair(2)
    ring_second(3)
    for number in range(7, 11):
        loads[number].wait()
    update(0)
    line_quad(2)
    line_pair(3)
    make_normed()
    update(1)
    line_quad(3)
    update(2)
    update(3)

    to_y = []
    for k in (2, 1, 3):
        other = lax.rem(y + k, 4)
        to_y.append(copies.send(w_out.at[other], w_all.at[:, y, x, core], y_peer[k]))
    for h in range(2):
        w_all[h, y, x, core] = w_out[y, h]
    for copy in to_y:
        copy.wait_recv()
    mine = w_all.at[:, :, x, core]
    to_x = [(k, copies.send(mine, mine, x_peer[k])) for k in (2, 1, 3)]
    to_core = [copies.send(mine, mine, sibling)]
    for k, copy in (to_x[1], to_x[2], to_x[0]):
        copy.wait_recv()
        theirs = w_all.at[:, :, lax.rem(x + 4 - k, 4), core]
        to_core.append(copies.send(theirs, theirs, sibling))
    for copy in to_core:
        copy.wait_recv()

    for h in range(2):
        key_part[h] = jnp.dot(
            normed[...], w_all[h].reshape(512, 128), preferred_element_type=F32
        ).reshape(8, 16, 128)
    to_z = []
    for k in (8, 7, 9, 6, 10, 5, 11, 4, 12, 3, 13, 2, 14, 1, 15):
        other = z_of(k)
        to_z.append(
            copies.send(
                key_part.at[lax.div(other, 8), lax.rem(other, 8)], key_in.at[z], z_peer(k)
            )
        )
    key_in[z] = key_part[zh, zl]
    for copy in to_z:
        copy.wait_recv()
    keys = key_in[0]
    for k in range(1, 16):
        keys = keys + key_in[k]
    keys = keys.astype(BF16)
    keys_out[...] = keys.astype(F32)

    new = (
        lax.dot_general(
            q32[...].astype(BF16), keys, (((1,), (1,)), ((), ())), preferred_element_type=F32
        )
        * scale
    )
    row = lax.broadcasted_iota(jnp.int32, (128, 16), 0)
    column = lax.broadcasted_iota(jnp.int32, (128, 16), 1)
    same_row = (row // 32) == (column % 4)
    earlier = (column // 4) <= ((row % 32) // 8)
    new = jnp.where(same_row & earlier & (column < 12), new, -jnp.inf)
    top = jnp.maximum(old_top[...], jnp.max(new, axis=1, keepdims=True))
    fade = jnp.exp(old_top[...] - top)
    new = jnp.exp(new - top)
    total = old_sum[...] * fade + jnp.sum(new, axis=1, keepdims=True)
    new_probs = (new / total).astype(BF16)
    share = fade / total
    attended = jnp.dot(new_probs, sv32[...].astype(BF16), preferred_element_type=F32)
    for r in range(4):
        rows = slice(32 * r, 32 * r + 32)
        probs = (old_exp[rows, :] * share[rows]).astype(BF16)
        att = attended[rows] + jnp.dot(probs, cv_v[r, 0], preferred_element_type=F32)
        for s in range(3):
            att_out[s, r] = att[8 * s : 8 * s + 8]

    for copy in copies.made:
        copy.wait_send()
    assert len(copies.made) == N_COPIES, len(copies.made)


def body(
    train_inputs,
    key_cotangent,
    master,
    moment_one,
    moment_two,
    step_inputs,
    decode_queries,
    step_values,
    cache_keys,
    cache_values,
    cache_lengths,
    norm_gain,
):
    anywhere = pl.BlockSpec(memory_space=pl.ANY)
    vmem = pl.BlockSpec(memory_space=pltpu.VMEM)
    owned = jax.ShapeDtypeStruct(master.shape, F32)
    new_master, new_one, new_two, keys, attended = pl.pallas_call(
        kernel,
        out_shape=(
            owned,
            owned,
            owned,
            jax.ShapeDtypeStruct((16, 128), F32),
            jax.ShapeDtypeStruct((3, 4, 8, 128), F32),
        ),
        in_specs=[anywhere] * 10 + [pl.BlockSpec(memory_space=pltpu.SMEM), anywhere],
        out_specs=(vmem,) * 5,
        scratch_shapes=[
            pltpu.VMEM((1024, 1024), BF16),
            pltpu.VMEM((1024, 1024), BF16),
            pltpu.VMEM((3, 1, 16, 1024), F32),
            pltpu.VMEM((3, 4, 1024), BF16),
            pltpu.VMEM((3, 4, 8, 128), BF16),
            pltpu.VMEM((3, 4, 1, 128), BF16),
            pltpu.VMEM((4, 1, 512, 128), BF16),
            pltpu.VMEM((4, 1, 512, 128), BF16),
            pltpu.VMEM((64, 128), F32),
            pltpu.VMEM((CHUNKS, 2, 8, 4, 16, CW), F32),
            pltpu.VMEM((CHUNKS, 8, 4, 16, CW), F32),
            pltpu.VMEM((CHUNKS, 6, 4, 16, CW), BF16),
            pltpu.VMEM((CHUNKS, 6, 4, 16, CW), BF16),
            pltpu.VMEM((CHUNKS, 8, 16, CW), F32),
            pltpu.VMEM((CHUNKS, 4, 16, CW), BF16),
            pltpu.VMEM((CHUNKS, 4, 16, CW), BF16),
            pltpu.VMEM((CHUNKS, 4, 16, CW), F32),
            pltpu.VMEM((CHUNKS, 4, 16, CW), BF16),
            pltpu.VMEM((CHUNKS, 3, 16, CW), BF16),
            pltpu.VMEM((16, 1024), F32),
            pltpu.VMEM((4, 8, 16, 128), BF16),
            pltpu.VMEM((8, 4, 16, 128), BF16),
            pltpu.VMEM((16, 1, 128), F32),
            pltpu.VMEM((128, 512), BF16),
            pltpu.VMEM((4, 2, 16, 128), BF16),
            pltpu.VMEM((2, 4, 4, 2, 16, 128), BF16),
            pltpu.VMEM((2, 8, 16, 128), F32),
            pltpu.VMEM((16, 16, 128), F32),
            pltpu.VMEM((128, 128), F32),
            pltpu.VMEM((128, 512), F32),
            pltpu.VMEM((128, 1), F32),
            pltpu.VMEM((128, 1), F32),
            pltpu.VMEM((16, 128), F32),
            pltpu.SemaphoreType.DMA((11,)),
            pltpu.SemaphoreType.DMA((N_COPIES,)),
            pltpu.SemaphoreType.DMA((N_COPIES,)),
        ],
        compiler_params=pltpu.CompilerParams(
            collective_id=0, has_side_effects=True, vmem_limit_bytes=48 << 20
        ),
        name="adam_decode",
    )(
        train_inputs,
        key_cotangent,
        master,
        moment_one,
        moment_two,
        step_inputs,
        decode_queries,
        step_values,
        cache_keys,
        cache_values,
        cache_lengths,
        norm_gain.reshape(64, 128),
    )
    new_keys = keys[:12].reshape(step_values.shape).astype(BF16)
    decoded = (step_inputs.astype(F32) + attended.reshape(step_inputs.shape)).astype(BF16)
    return new_master, new_one, new_two, new_keys, decoded


def solution(mesh):
    return jax.shard_map(
        body,
        mesh=mesh,
        in_specs=(
            P("fsdp", "tp"),
            P("fsdp", None),
            P("tp", "fsdp", None),
            P("tp", "fsdp", None),
            P("tp", "fsdp", None),
            P(None, "fsdp", "tp"),
            P(None, "fsdp", "tp", None),
            P(None, "fsdp", "tp", None),
            P("fsdp", "tp", None, None),
            P("fsdp", "tp", None, None),
            P("fsdp"),
            P(),
        ),
        out_specs=(
            P("tp", "fsdp", None),
            P("tp", "fsdp", None),
            P("tp", "fsdp", None),
            P(None, "fsdp", "tp", None),
            P(None, "fsdp", "tp"),
        ),
        check_vma=False,
    )
```

```python
import functools

import jax
import jax.numpy as jnp
from jax import lax
from jax.experimental import pallas as pl
from jax.experimental.pallas import tpu as pltpu
from jax.sharding import PartitionSpec as P

MESH = pl.DeviceIdType.MESH
correction_one = 1.0 - 0.9**4
correction_two = 1.0 - 0.95**4

CHUNKS = 4
CW = 1024 // CHUNKS
F32 = jnp.float32
BF16 = jnp.bfloat16


class Copies:
    def __init__(self, send_sems, recv_sems):
        self.send_sems, self.recv_sems = send_sems, recv_sems
        self.made = []

    def send(self, src, dst, device, recv_sem=None):
        number = len(self.made)
        copy = pltpu.make_async_remote_copy(
            src_ref=src,
            dst_ref=dst,
            send_sem=self.send_sems.at[number],
            recv_sem=self.recv_sems.at[number] if recv_sem is None else recv_sem,
            device_id=device,
            device_id_type=MESH,
        )
        copy.start()
        self.made.append(copy)
        return copy


N_COPIES = 25 + 11 * CHUNKS + 35


def kernel(
    x_hbm,
    c_hbm,
    master_hbm,
    one_hbm,
    two_hbm,
    step_hbm,
    query_hbm,
    value_hbm,
    ck_hbm,
    cv_hbm,
    lengths,
    gain_hbm,
    new_master,
    new_one,
    new_two,
    keys_out,
    att_out,
    x_v,
    c_v,
    adam_v,
    step_v,
    query_v,
    value_v,
    ck_v,
    cv_v,
    gain_v,
    part,
    part_in,
    ring_out,
    ring_in,
    line_sum,
    pair_out,
    pair_in,
    quad_sum,
    quad_out,
    quad_in,
    rows32,
    rows_y,
    rows_z,
    squares,
    normed,
    w_out,
    w_all,
    key_part,
    key_in,
    q32,
    old_exp,
    old_top,
    old_sum,
    sv32,
    local_sems,
    send_sems,
    recv_sems,
    key_sems,
    far_sems,
):
    f, t = lax.axis_index("fsdp"), lax.axis_index("tp")
    core = lax.rem(f, 2)
    x = lax.rem(lax.div(f, 2), 4)
    zl = lax.div(f, 8)
    y = lax.rem(t, 4)
    zh = lax.div(t, 4)
    z = zh * 8 + zl

    def fsdp(zl_, x_, core_):
        return (zl_ * 4 + x_) * 2 + core_

    def at(zl_=zl, x_=x, core_=core, zh_=zh, y_=y):
        return {"fsdp": fsdp(zl_, x_, core_), "tp": zh_ * 4 + y_}

    sibling = at(core_=1 - core)
    x_peer = [None] + [at(x_=lax.rem(x + k, 4)) for k in (1, 2, 3)]
    y_peer = [None] + [at(y_=lax.rem(y + k, 4)) for k in (1, 2, 3)]

    def z_of(k):
        return lax.rem(z + k, 16)

    def z_peer(k):
        other = z_of(k)
        return at(zl_=lax.rem(other, 8), zh_=lax.div(other, 8))

    barrier = pltpu.get_barrier_semaphore()
    group = [sibling] + [
        at(x_=lax.rem(x + k, 4), core_=c_) for k in (2, 1, 3) for c_ in (core, 1 - core)
    ]
    partners = group + y_peer[1:] + [z_peer(1), z_peer(15)]
    for partner in partners:
        pl.semaphore_signal(barrier, inc=1, device_id=partner, device_id_type=MESH)

    loads = []
    for number, (src, dst) in enumerate(
        (
            (x_hbm, x_v),
            (c_hbm, c_v),
            (step_hbm, step_v),
            (query_hbm, query_v),
            (ck_hbm, ck_v),
            (cv_hbm, cv_v),
            (value_hbm, value_v),
            (gain_hbm, gain_v),
            (master_hbm, adam_v.at[0]),
            (one_hbm, adam_v.at[1]),
            (two_hbm, adam_v.at[2]),
        )
    ):
        load = pltpu.make_async_copy(src, dst, local_sems.at[number])
        load.start()
        loads.append(load)

    loads[2].wait()
    rows32[...] = jnp.zeros_like(rows32)
    for s in range(3):
        rows32[4 * s : 4 * s + 4, :] = step_v[s].astype(F32)
    for k in range(8):
        rows_y[y, k] = rows32[:, 128 * k : 128 * k + 128].astype(BF16)

    pl.semaphore_wait(barrier, len(partners))
    copies = Copies(send_sems, recv_sems)

    def hop(d):
        if d > 0:
            pl.semaphore_wait(far_sems.at[d - 1, 0], 1)
            pl.semaphore_wait(far_sems.at[d - 1, 1], 1)
        if d < 7:
            for side, partner in enumerate((z_peer(1), z_peer(15))):
                pl.semaphore_signal(
                    far_sems.at[d, side], inc=1, device_id=partner, device_id_type=MESH
                )

    hop(0)
    own_rows = [copies.send(rows_y.at[y], rows_y.at[y], y_peer[k]) for k in (2, 1, 3)]

    loads[0].wait()
    loads[1].wait()
    swaps = []
    for j in range(CHUNKS):
        term = lax.dot_general(
            x_v[...],
            c_v[:, j * CW : (j + 1) * CW],
            (((0,), (0,)), ((), ())),
            preferred_element_type=F32,
        ).reshape(8, 4, 2, 16, CW)
        part[j, 0] = term[:, :, 0]
        part[j, 1] = term[:, :, 1]
        swaps.append(copies.send(part.at[j, 1 - core], part_in.at[j], sibling))
        hop(j + 1)

    xp, xo, xm = (lax.rem(x + k, 4) for k in (1, 2, 3))
    low, high = slice(0, 4), slice(4, 8)
    ring, pairs, quads = {}, {}, {}
    parity, quad = lax.rem(zl, 2), lax.div(zl, 2)

    def chip_sum(j, half, target):
        return part[j, core, half, target] + part_in[j, half, target]

    def ring_send(j, number, value, device):
        ring_out[j, number] = value.astype(BF16)
        ring[j, number] = copies.send(ring_out.at[j, number], ring_in.at[j, number], device)

    def ring_first(j):
        swaps[j].wait_recv()
        ring_send(j, 0, chip_sum(j, low, xo), x_peer[1])
        ring_send(j, 1, chip_sum(j, high, xo), x_peer[3])
        ring_send(j, 2, chip_sum(j, high, xp), x_peer[1])
        ring_send(j, 3, chip_sum(j, low, xm), x_peer[3])

    def ring_second(j):
        ring[j, 0].wait_recv()
        ring_send(j, 4, chip_sum(j, low, xp) + ring_in[j, 0].astype(F32), x_peer[1])
        ring[j, 1].wait_recv()
        ring_send(j, 5, chip_sum(j, high, xm) + ring_in[j, 1].astype(F32), x_peer[3])

    def line_pair(j):
        for number in (2, 3, 4, 5):
            ring[j, number].wait_recv()
        line_sum[j, low] = (
            chip_sum(j, low, x) + ring_in[j, 3].astype(F32) + ring_in[j, 4].astype(F32)
        )
        line_sum[j, high] = (
            chip_sum(j, high, x) + ring_in[j, 2].astype(F32) + ring_in[j, 5].astype(F32)
        )
        for q in range(4):
            pair_out[j, q] = line_sum[j, 2 * q + 1 - parity].astype(BF16)
        pairs[j] = copies.send(
            pair_out.at[j], pair_in.at[j], at(zl_=zl + 1 - 2 * parity)
        )

    def line_quad(j):
        pairs[j].wait_recv()
        for q in range(4):
            total = line_sum[j, 2 * q + parity] + pair_in[j, q].astype(F32)
            quad_sum[j, q] = total
            quad_out[j, q] = total.astype(BF16)
        for k in (2, 3, 1):
            other = lax.rem(quad + k, 4)
            quads[j, k] = copies.send(
                quad_out.at[j, other], quad_in.at[j, k - 1], at(zl_=2 * other + parity)
            )

    def update(j):
        for k in (1, 2, 3):
            quads[j, k].wait_recv()
        gradient = quad_sum[j, quad]
        for k in (1, 2, 3):
            gradient = gradient + quad_in[j, k - 1].astype(F32)
        columns = slice(j * CW, (j + 1) * CW)
        one = 0.9 * adam_v[1, 0, :, columns] + 0.1 * gradient
        two = 0.95 * adam_v[2, 0, :, columns] + 0.05 * gradient * gradient
        fresh = adam_v[0, 0, :, columns] - 0.003 * (one / correction_one) / (
            jnp.sqrt(two / correction_two) + 1e-08
        )
        new_one[0, :, columns] = one
        new_two[0, :, columns] = two
        new_master[0, :, columns] = fresh
        weights = fresh.astype(BF16)
        for k in range(CW // 128):
            head = j * (CW // 128) + k
            w_out[head // 4, head % 4] = weights[:, 128 * k : 128 * k + 128]

    lane = lax.broadcasted_iota(jnp.int32, (16, 128), 1)
    diagonal = lane == lax.broadcasted_iota(jnp.int32, (16, 128), 0)
    spread, rows_sent = {}, {}

    def send_rows():
        for copy in own_rows:
            copy.wait_recv()
        for k in (4, 3, 5, 2, 6, 1, 7):
            other = lax.rem(zl + k, 8)
            rows_sent[k] = copies.send(rows_y.at[:, other], rows_z.at[zl], at(zl_=other))
        total = jnp.zeros((16, 128), F32)
        for q in range(4):
            for k in range(8):
                block = rows_y[q, k].astype(F32)
                total = total + block * block
        column = jnp.sum(total, axis=1, keepdims=True)
        squares[z] = jnp.sum(jnp.where(diagonal, column, 0.0), axis=0, keepdims=True)
        for k in (8, 7, 9, 6, 10, 5, 11, 4, 12, 3, 13, 2, 14, 1, 15):
            spread[k] = copies.send(squares.at[z], squares.at[z], z_peer(k))
        for q in range(4):
            rows_z[zl, q] = rows_y[q, zl]

    def make_normed():
        for k in range(1, 16):
            spread[k].wait_recv()
        for k in range(1, 8):
            rows_sent[k].wait_recv()
        for s in range(8):
            both = squares[s] + squares[s + 8]
            column = jnp.sum(jnp.where(diagonal, both, 0.0), axis=1, keepdims=True)
            inverse = lax.rsqrt(column * (1.0 / 8192.0) + 1e-06)
            for q in range(4):
                gain = gain_v[pl.ds((zh * 4 + q) * 8 + zl, 1), :]
                block = rows_z[s, q].astype(F32) * inverse * gain
                normed[16 * s : 16 * s + 16, 128 * q : 128 * q + 128] = block.astype(BF16)

    scale = 1.0 / 128.0**0.5

    def old_scores():
        for number in (3, 4, 5, 6):
            loads[number].wait()
        q32[...] = jnp.zeros_like(q32)
        for s in range(3):
            for r in range(4):
                q32[32 * r + 8 * s : 32 * r + 8 * s + 8, :] = query_v[s, r].astype(F32)
        sv32[...] = jnp.zeros_like(sv32)
        for s in range(3):
            sv32[4 * s : 4 * s + 4, :] = value_v[s].astype(F32)
        slot = lax.broadcasted_iota(jnp.int32, (32, 512), 1)
        for r in range(4):
            scores = (
                lax.dot_general(
                    q32[32 * r : 32 * r + 32, :].astype(BF16),
                    ck_v[r, 0],
                    (((1,), (1,)), ((), ())),
                    preferred_element_type=F32,
                )
                * scale
            )
            scores = jnp.where(slot < lengths[r], scores, -jnp.inf)
            top = jnp.max(scores, axis=1, keepdims=True)
            weight = jnp.exp(scores - top)
            rows = slice(32 * r, 32 * r + 32)
            old_exp[rows, :] = weight
            old_top[rows, :] = top
            old_sum[rows, :] = jnp.sum(weight, axis=1, keepdims=True)

    to_y, to_group, to_z = {}, {}, []

    def head_columns(h):
        to_y[h] = [
            copies.send(
                w_out.at[h, lax.rem(y + k, 4)], w_all.at[h, y, x, core], y_peer[k]
            )
            for k in (2, 1, 3)
        ]
        w_all[h, y, x, core] = w_out[h, y]

    def share_weights(h):
        for copy in to_y[h]:
            copy.wait_recv()
        mine = w_all.at[h, :, x, core]
        to_group[h] = [copies.send(mine, mine, device) for device in group[1:] + group[:1]]

    def send_keys(h):
        for copy in to_group[h]:
            copy.wait_recv()
        key_part[h] = jnp.dot(
            normed[...], w_all[h].reshape(512, 128), preferred_element_type=F32
        ).reshape(8, 16, 128)
        away = zh if h == 0 else 1 - zh
        if h == 1:
            copies.send(
                key_part.at[1 - zh, zl, pl.ds(0, 12)],
                key_in.at[z, pl.ds(0, 12)],
                at(zh_=1 - zh),
                key_sems.at[14],
            )
        for k in (4, 3, 5, 2, 6, 1, 7):
            other = lax.rem(zl + k, 8)
            copies.send(
                key_part.at[h, other, pl.ds(0, 12)],
                key_in.at[z, pl.ds(0, 12)],
                at(zl_=other, zh_=h),
                key_sems.at[away * 7 + k - 1],
            )

    def finish():
        key_in[z] = key_part[zh, zl]
        for number in range(15):
            pltpu.make_async_remote_copy(
                src_ref=key_part.at[0, 0, pl.ds(0, 12)],
                dst_ref=key_in.at[0, pl.ds(0, 12)],
                send_sem=send_sems.at[0],
                recv_sem=key_sems.at[number],
                device_id=sibling,
                device_id_type=MESH,
            ).wait_recv()
        total = key_in[0, 0:12]
        for k in range(1, 16):
            total = total + key_in[k, 0:12]
        keys_out[...] = jnp.zeros_like(keys_out)
        keys_out[0:12, :] = total
        keys = keys_out[...].astype(BF16)

        new = (
            lax.dot_general(
                q32[...].astype(BF16), keys, (((1,), (1,)), ((), ())), preferred_element_type=F32
            )
            * scale
        )
        row = lax.broadcasted_iota(jnp.int32, (128, 16), 0)
        column = lax.broadcasted_iota(jnp.int32, (128, 16), 1)
        same_row = (row // 32) == (column % 4)
        earlier = (column // 4) <= ((row % 32) // 8)
        new = jnp.where(same_row & earlier & (column < 12), new, -jnp.inf)
        top = jnp.maximum(old_top[...], jnp.max(new, axis=1, keepdims=True))
        fade = jnp.exp(old_top[...] - top)
        new = jnp.exp(new - top)
        total = old_sum[...] * fade + jnp.sum(new, axis=1, keepdims=True)
        new_probs = (new / total).astype(BF16)
        share = fade / total
        attended = jnp.dot(new_probs, sv32[...].astype(BF16), preferred_element_type=F32)
        for r in range(4):
            rows = slice(32 * r, 32 * r + 32)
            probs = (old_exp[rows, :] * share[rows]).astype(BF16)
            att = attended[rows] + jnp.dot(probs, cv_v[r, 0], preferred_element_type=F32)
            for s in range(3):
                att_out[s, r] = att[8 * s : 8 * s + 8]

    def adam_loads():
        for number in range(7, 11):
            loads[number].wait()

    schedule = (
        (ring_first, 0),
        (hop, 5),
        (ring_first, 1),
        (ring_second, 0),
        (hop, 6),
        (line_pair, 0),
        (ring_first, 2),
        (hop, 7),
        (send_rows,),
        (ring_second, 1),
        (line_quad, 0),
        (line_pair, 1),
        (ring_first, 3),
        (ring_second, 2),
        (line_quad, 1),
        (line_pair, 2),
        (ring_second, 3),
        (adam_loads,),
        (update, 0),
        (line_quad, 2),
        (line_pair, 3),
        (update, 1),
        (head_columns, 0),
        (line_quad, 3),
        (share_weights, 0),
        (make_normed,),
        (update, 2),
        (send_keys, 0),
        (update, 3),
        (head_columns, 1),
        (old_scores,),
        (share_weights, 1),
        (send_keys, 1),
        (finish,),
    )
    for do, *chunk in schedule:
        do(*chunk)

    for copy in copies.made:
        copy.wait_send()
    assert len(copies.made) == N_COPIES, len(copies.made)


def store(
    master_v, one_v, two_v, keys_v, att_v, step_v, master, one, two, keys, decoded, keys_b, dec_b, sems
):
    copies = []

    def start(src, dst):
        copies.append(pltpu.make_async_copy(src, dst, sems.at[len(copies)]))
        copies[-1].start()

    start(master_v, master)
    start(one_v, one)
    start(two_v, two)
    for s in range(3):
        keys_b[s] = keys_v[4 * s : 4 * s + 4, :].astype(BF16)
    start(keys_b, keys)
    for s in range(3):
        for g in range(8):
            columns = slice(128 * g, 128 * g + 128)
            dec_b[s, :, columns] = (
                step_v[s, :, columns].astype(F32) + att_v[s, :, g, :]
            ).astype(BF16)
    start(dec_b, decoded)
    for copy in copies:
        copy.wait()


def body(
    train_inputs,
    key_cotangent,
    master,
    moment_one,
    moment_two,
    step_inputs,
    decode_queries,
    step_values,
    cache_keys,
    cache_values,
    cache_lengths,
    norm_gain,
):
    hbm = pl.BlockSpec(memory_space=pltpu.HBM)
    vmem = pl.BlockSpec(memory_space=pltpu.VMEM)
    owned = jax.ShapeDtypeStruct(master.shape, F32)
    owned_v = pltpu.VMEM(master.shape, F32)
    results = pl.pallas_call(
        kernel,
        out_shape=(
            owned_v,
            owned_v,
            owned_v,
            pltpu.VMEM((16, 128), F32),
            pltpu.VMEM((3, 4, 8, 128), F32),
        ),
        in_specs=[hbm] * 10 + [pl.BlockSpec(memory_space=pltpu.SMEM), hbm],
        out_specs=(vmem,) * 5,
        scratch_shapes=[
            pltpu.VMEM((1024, 1024), BF16),
            pltpu.VMEM((1024, 1024), BF16),
            pltpu.VMEM((3, 1, 16, 1024), F32),
            pltpu.VMEM((3, 4, 1024), BF16),
            pltpu.VMEM((3, 4, 8, 128), BF16),
            pltpu.VMEM((3, 4, 128), BF16),
            pltpu.VMEM((4, 1, 512, 128), BF16),
            pltpu.VMEM((4, 1, 512, 128), BF16),
            pltpu.VMEM((64, 128), F32),
            pltpu.VMEM((CHUNKS, 2, 8, 4, 16, CW), F32),
            pltpu.VMEM((CHUNKS, 8, 4, 16, CW), F32),
            pltpu.VMEM((CHUNKS, 6, 4, 16, CW), BF16),
            pltpu.VMEM((CHUNKS, 6, 4, 16, CW), BF16),
            pltpu.VMEM((CHUNKS, 8, 16, CW), F32),
            pltpu.VMEM((CHUNKS, 4, 16, CW), BF16),
            pltpu.VMEM((CHUNKS, 4, 16, CW), BF16),
            pltpu.VMEM((CHUNKS, 4, 16, CW), F32),
            pltpu.VMEM((CHUNKS, 4, 16, CW), BF16),
            pltpu.VMEM((CHUNKS, 3, 16, CW), BF16),
            pltpu.VMEM((16, 1024), F32),
            pltpu.VMEM((4, 8, 16, 128), BF16),
            pltpu.VMEM((8, 4, 16, 128), BF16),
            pltpu.VMEM((16, 1, 128), F32),
            pltpu.VMEM((128, 512), BF16),
            pltpu.VMEM((2, 4, 16, 128), BF16),
            pltpu.VMEM((2, 4, 4, 2, 16, 128), BF16),
            pltpu.VMEM((2, 8, 16, 128), F32),
            pltpu.VMEM((16, 16, 128), F32),
            pltpu.VMEM((128, 128), F32),
            pltpu.VMEM((128, 512), F32),
            pltpu.VMEM((128, 1), F32),
            pltpu.VMEM((128, 1), F32),
            pltpu.VMEM((16, 128), F32),
            pltpu.SemaphoreType.DMA((11,)),
            pltpu.SemaphoreType.DMA((N_COPIES,)),
            pltpu.SemaphoreType.DMA((N_COPIES,)),
            pltpu.SemaphoreType.DMA((15,)),
            pltpu.SemaphoreType.REGULAR((7, 2)),
        ],
        compiler_params=pltpu.CompilerParams(
            collective_id=0, has_side_effects=True, vmem_limit_bytes=40 << 20
        ),
        name="adam_decode",
    )(
        *(
            pltpu.with_memory_space_constraint(array, pltpu.HBM)
            for array in (
                train_inputs,
                key_cotangent,
                master,
                moment_one,
                moment_two,
                step_inputs,
                decode_queries,
                step_values.reshape(3, 4, 128),
                cache_keys,
                cache_values,
            )
        ),
        cache_lengths,
        pltpu.with_memory_space_constraint(norm_gain.reshape(64, 128), pltpu.HBM),
    )
    new_master, new_one, new_two, new_keys, decoded = pl.pallas_call(
        store,
        out_shape=(
            owned,
            owned,
            owned,
            jax.ShapeDtypeStruct((3, 4, 128), BF16),
            jax.ShapeDtypeStruct(step_inputs.shape, BF16),
        ),
        in_specs=[vmem] * 6,
        out_specs=(hbm,) * 5,
        scratch_shapes=[
            pltpu.VMEM((3, 4, 128), BF16),
            pltpu.VMEM((3, 4, 1024), BF16),
            pltpu.SemaphoreType.DMA((5,)),
        ],
        compiler_params=pltpu.CompilerParams(vmem_limit_bytes=40 << 20),
        name="store_results",
    )(*results, step_inputs)
    return new_master, new_one, new_two, new_keys.reshape(step_values.shape), decoded


def solution(mesh):
    return jax.shard_map(
        body,
        mesh=mesh,
        in_specs=(
            P("fsdp", "tp"),
            P("fsdp", None),
            P("tp", "fsdp", None),
            P("tp", "fsdp", None),
            P("tp", "fsdp", None),
            P(None, "fsdp", "tp"),
            P(None, "fsdp", "tp", None),
            P(None, "fsdp", "tp", None),
            P("fsdp", "tp", None, None),
            P("fsdp", "tp", None, None),
            P("fsdp"),
            P(),
        ),
        out_specs=(
            P("tp", "fsdp", None),
            P("tp", "fsdp", None),
            P("tp", "fsdp", None),
            P(None, "fsdp", "tp", None),
            P(None, "fsdp", "tp"),
        ),
        check_vma=False,
    )
```

```python
import functools

import jax
import jax.numpy as jnp
from jax import lax
from jax.experimental import pallas as pl
from jax.experimental.pallas import tpu as pltpu
from jax.sharding import PartitionSpec as P

MESH = pl.DeviceIdType.MESH
correction_one = 1.0 - 0.9**4
correction_two = 1.0 - 0.95**4

CHUNKS = 4
CW = 1024 // CHUNKS
F32 = jnp.float32
BF16 = jnp.bfloat16


class Sems:
    def __init__(self, sems):
        self.sems, self.used = sems, 0

    def new(self):
        self.used += 1
        return self.sems.at[self.used - 1]


def remote(src, dst, send_sem, recv_sem, device):
    return pltpu.make_async_remote_copy(
        src_ref=src,
        dst_ref=dst,
        send_sem=send_sem,
        recv_sem=recv_sem,
        device_id=device,
        device_id_type=MESH,
    )


N_SEMS = 27 + 7 * CHUNKS


def kernel(
    x_hbm,
    c_hbm,
    master_hbm,
    one_hbm,
    two_hbm,
    step_hbm,
    query_hbm,
    value_hbm,
    ck_hbm,
    cv_hbm,
    lengths,
    gain_hbm,
    new_master,
    new_one,
    new_two,
    keys_out,
    att_out,
    x_v,
    c_v,
    adam_v,
    step_v,
    query_v,
    value_v,
    ck_v,
    cv_v,
    gain_v,
    part,
    part_in,
    ring_out,
    ring_in,
    line_sum,
    pair_out,
    pair_in,
    quad_sum,
    quad_out,
    quad_in,
    rows32,
    rows_y,
    rows_z,
    squares,
    normed,
    w_out,
    w_all,
    key_part,
    key_in,
    q32,
    old_exp,
    old_top,
    old_sum,
    sv32,
    copy_sems,
    far_sems,
):
    f, t = lax.axis_index("fsdp"), lax.axis_index("tp")
    core = lax.rem(f, 2)
    x = lax.rem(lax.div(f, 2), 4)
    zl = lax.div(f, 8)
    y = lax.rem(t, 4)
    zh = lax.div(t, 4)
    z = zh * 8 + zl

    def fsdp(zl_, x_, core_):
        return (zl_ * 4 + x_) * 2 + core_

    def at(zl_=zl, x_=x, core_=core, zh_=zh, y_=y):
        return {"fsdp": fsdp(zl_, x_, core_), "tp": zh_ * 4 + y_}

    sibling = at(core_=1 - core)
    x_peer = [None] + [at(x_=lax.rem(x + k, 4)) for k in (1, 2, 3)]
    y_peer = [None] + [at(y_=lax.rem(y + k, 4)) for k in (1, 2, 3)]

    def z_of(k):
        return lax.rem(z + k, 16)

    def z_peer(k):
        other = z_of(k)
        return at(zl_=lax.rem(other, 8), zh_=lax.div(other, 8))

    sems = Sems(copy_sems)

    barrier = pltpu.get_barrier_semaphore()
    group = [sibling] + [
        at(x_=lax.rem(x + k, 4), core_=c_) for k in (2, 1, 3) for c_ in (core, 1 - core)
    ]
    partners = group + y_peer[1:] + [z_peer(1), z_peer(15)]
    for partner in partners:
        pl.semaphore_signal(barrier, inc=1, device_id=partner, device_id_type=MESH)

    def load(pairs, whole=None):
        sem = sems.new()
        for src, dst in pairs:
            pltpu.make_async_copy(src, dst, sem).start()
        return pltpu.make_async_copy(*(whole or pairs[0]), sem)

    step_load = load([(step_hbm, step_v)])
    x_load = load([(x_hbm, x_v)])
    c_loads = []
    for j in range(CHUNKS):
        columns = slice(j * CW, (j + 1) * CW)
        c_loads.append(load([(c_hbm.at[:, columns], c_v.at[:, columns])]))
    score_loads = [
        load([pair])
        for pair in ((query_hbm, query_v), (ck_hbm, ck_v), (cv_hbm, cv_v), (value_hbm, value_v))
    ]
    gain_load = load([(gain_hbm, gain_v)])
    adam_load = load(
        [(ref, adam_v.at[k]) for k, ref in enumerate((master_hbm, one_hbm, two_hbm))],
        (adam_v, adam_v),
    )

    step_load.wait()
    rows32[...] = jnp.zeros_like(rows32)
    for s in range(3):
        rows32[4 * s : 4 * s + 4, :] = step_v[s].astype(F32)
    for k in range(8):
        rows_y[y, k] = rows32[:, 128 * k : 128 * k + 128].astype(BF16)

    pl.semaphore_wait(barrier, len(partners))
    sent = []

    def sender(whole):
        sem = sems.new()
        sent.append(remote(whole, whole, sem, sem, sibling))
        return sem

    def arrival(whole):
        sem = sems.new()
        return sem, remote(whole, whole, sem, sem, sibling)

    def hop(d):
        if d > 0:
            pl.semaphore_wait(far_sems.at[d - 1], 2)
        if d < 7:
            for partner in (z_peer(1), z_peer(15)):
                pl.semaphore_signal(
                    far_sems.at[d], inc=1, device_id=partner, device_id_type=MESH
                )

    hop(0)
    own_sent, (own_sem, own_rows) = sender(rows_y.at[0:3]), arrival(rows_y.at[0:3])
    for k in (2, 1, 3):
        remote(rows_y.at[y], rows_y.at[y], own_sent, own_sem, y_peer[k]).start()

    swap_sent = sender(part.at[:, 1 - core])
    swaps = [arrival(part_in.at[j]) for j in range(CHUNKS)]

    def local_term(j):
        if j == 0:
            x_load.wait()
        c_loads[j].wait()
        term = lax.dot_general(
            x_v[...],
            c_v[:, j * CW : (j + 1) * CW],
            (((0,), (0,)), ((), ())),
            preferred_element_type=F32,
        ).reshape(8, 4, 2, 16, CW)
        part[j, 0] = term[:, :, 0]
        part[j, 1] = term[:, :, 1]
        remote(part.at[j, 1 - core], part_in.at[j], swap_sent, swaps[j][0], sibling).start()

    xp, xo, xm = (lax.rem(x + k, 4) for k in (1, 2, 3))
    low, high = slice(0, 4), slice(4, 8)
    ring_sent = sender(ring_out)
    ring = [
        [arrival(ring_in.at[j, 0]), arrival(ring_in.at[j, 1])]
        + [arrival(ring_in.at[j, 2:6])] * 4
        for j in range(CHUNKS)
    ]
    pair_sent = sender(pair_out)
    pairs = [arrival(pair_in.at[j]) for j in range(CHUNKS)]
    quad_sent = sender(quad_out.at[:, 0:3])
    quads = [arrival(quad_in.at[j]) for j in range(CHUNKS)]
    parity, quad = lax.rem(zl, 2), lax.div(zl, 2)

    def chip_sum(j, half, target):
        return part[j, core, half, target] + part_in[j, half, target]

    def ring_send(j, number, value, device):
        ring_out[j, number] = value.astype(BF16)
        remote(
            ring_out.at[j, number], ring_in.at[j, number], ring_sent, ring[j][number][0], device
        ).start()

    def ring_first(j):
        swaps[j][1].wait_recv()
        ring_send(j, 0, chip_sum(j, low, xo), x_peer[1])
        ring_send(j, 1, chip_sum(j, high, xo), x_peer[3])
        ring_send(j, 2, chip_sum(j, high, xp), x_peer[1])
        ring_send(j, 3, chip_sum(j, low, xm), x_peer[3])

    def ring_second(j):
        ring[j][0][1].wait_recv()
        ring_send(j, 4, chip_sum(j, low, xp) + ring_in[j, 0].astype(F32), x_peer[1])
        ring[j][1][1].wait_recv()
        ring_send(j, 5, chip_sum(j, high, xm) + ring_in[j, 1].astype(F32), x_peer[3])

    def line_pair(j):
        ring[j][2][1].wait_recv()
        line_sum[j, low] = (
            chip_sum(j, low, x) + ring_in[j, 3].astype(F32) + ring_in[j, 4].astype(F32)
        )
        line_sum[j, high] = (
            chip_sum(j, high, x) + ring_in[j, 2].astype(F32) + ring_in[j, 5].astype(F32)
        )
        for q in range(4):
            pair_out[j, q] = line_sum[j, 2 * q + 1 - parity].astype(BF16)
        remote(
            pair_out.at[j], pair_in.at[j], pair_sent, pairs[j][0], at(zl_=zl + 1 - 2 * parity)
        ).start()

    def line_quad(j):
        pairs[j][1].wait_recv()
        for q in range(4):
            total = line_sum[j, 2 * q + parity] + pair_in[j, q].astype(F32)
            quad_sum[j, q] = total
            quad_out[j, q] = total.astype(BF16)
        for k in (2, 3, 1):
            other = lax.rem(quad + k, 4)
            remote(
                quad_out.at[j, other],
                quad_in.at[j, k - 1],
                quad_sent,
                quads[j][0],
                at(zl_=2 * other + parity),
            ).start()

    def update(j):
        quads[j][1].wait_recv()
        gradient = quad_sum[j, quad]
        for k in (1, 2, 3):
            gradient = gradient + quad_in[j, k - 1].astype(F32)
        columns = slice(j * CW, (j + 1) * CW)
        one = 0.9 * adam_v[1, 0, :, columns] + 0.1 * gradient
        two = 0.95 * adam_v[2, 0, :, columns] + 0.05 * gradient * gradient
        fresh = adam_v[0, 0, :, columns] - 0.003 * (one / correction_one) / (
            jnp.sqrt(two / correction_two) + 1e-08
        )
        new_one[0, :, columns] = one
        new_two[0, :, columns] = two
        new_master[0, :, columns] = fresh
        weights = fresh.astype(BF16)
        for k in range(CW // 128):
            head = j * (CW // 128) + k
            w_out[head // 4, head % 4] = weights[:, 128 * k : 128 * k + 128]

    lane = lax.broadcasted_iota(jnp.int32, (16, 128), 1)
    diagonal = lane == lax.broadcasted_iota(jnp.int32, (16, 128), 0)
    rows_sent, (rows_sem, rows_here) = sender(rows_z.at[0:7]), arrival(rows_z.at[0:7])
    squares_sent, (squares_sem, squares_here) = (
        sender(squares.at[0:15]),
        arrival(squares.at[0:15]),
    )

    def send_rows():
        own_rows.wait_recv()
        for k in (4, 3, 5, 2, 6, 1, 7):
            other = lax.rem(zl + k, 8)
            remote(
                rows_y.at[:, other], rows_z.at[zl], rows_sent, rows_sem, at(zl_=other)
            ).start()
        total = jnp.zeros((16, 128), F32)
        for q in range(4):
            for k in range(8):
                block = rows_y[q, k].astype(F32)
                total = total + block * block
        column = jnp.sum(total, axis=1, keepdims=True)
        squares[z] = jnp.sum(jnp.where(diagonal, column, 0.0), axis=0, keepdims=True)
        for k in (8, 7, 9, 6, 10, 5, 11, 4, 12, 3, 13, 2, 14, 1, 15):
            remote(squares.at[z], squares.at[z], squares_sent, squares_sem, z_peer(k)).start()
        for q in range(4):
            rows_z[zl, q] = rows_y[q, zl]

    def make_normed():
        gain_load.wait()
        squares_here.wait_recv()
        rows_here.wait_recv()
        for s in range(8):
            both = squares[s] + squares[s + 8]
            column = jnp.sum(jnp.where(diagonal, both, 0.0), axis=1, keepdims=True)
            inverse = lax.rsqrt(column * (1.0 / 8192.0) + 1e-06)
            for q in range(4):
                gain = gain_v[pl.ds((zh * 4 + q) * 8 + zl, 1), :]
                block = rows_z[s, q].astype(F32) * inverse * gain
                normed[16 * s : 16 * s + 16, 128 * q : 128 * q + 128] = block.astype(BF16)

    scale = 1.0 / 128.0**0.5

    def old_scores():
        for copy in score_loads:
            copy.wait()
        q32[...] = jnp.zeros_like(q32)
        for s in range(3):
            for r in range(4):
                q32[32 * r + 8 * s : 32 * r + 8 * s + 8, :] = query_v[s, r].astype(F32)
        sv32[...] = jnp.zeros_like(sv32)
        for s in range(3):
            sv32[4 * s : 4 * s + 4, :] = value_v[s].astype(F32)
        slot = lax.broadcasted_iota(jnp.int32, (32, 512), 1)
        for r in range(4):
            scores = (
                lax.dot_general(
                    q32[32 * r : 32 * r + 32, :].astype(BF16),
                    ck_v[r, 0],
                    (((1,), (1,)), ((), ())),
                    preferred_element_type=F32,
                )
                * scale
            )
            scores = jnp.where(slot < lengths[r], scores, -jnp.inf)
            top = jnp.max(scores, axis=1, keepdims=True)
            weight = jnp.exp(scores - top)
            rows = slice(32 * r, 32 * r + 32)
            old_exp[rows, :] = weight
            old_top[rows, :] = top
            old_sum[rows, :] = jnp.sum(weight, axis=1, keepdims=True)

    to_y_sent = sender(w_out.at[:, 0:3])
    to_y = [arrival(w_out.at[h, 0:3]) for h in range(2)]
    shared_sent = [sender(rows_z.at[0:7]) for h in range(2)]
    shared = [arrival(rows_z.at[0:7]) for h in range(2)]
    keys_sent = sender(key_in.at[0:15, pl.ds(0, 12)])
    keys_sem, keys_here = arrival(key_in.at[0:15, pl.ds(0, 12)])

    def head_columns(h):
        for k in (2, 1, 3):
            remote(
                w_out.at[h, lax.rem(y + k, 4)],
                w_all.at[h, y, x, core],
                to_y_sent,
                to_y[h][0],
                y_peer[k],
            ).start()
        w_all[h, y, x, core] = w_out[h, y]

    def share_weights(h):
        to_y[h][1].wait_recv()
        mine = w_all.at[h, :, x, core]
        for device in group[1:] + group[:1]:
            remote(mine, mine, shared_sent[h], shared[h][0], device).start()

    def send_keys(h):
        shared[h][1].wait_recv()
        key_part[h] = jnp.dot(
            normed[...], w_all[h].reshape(512, 128), preferred_element_type=F32
        ).reshape(8, 16, 128)

        def send(half, line):
            remote(
                key_part.at[half, line, pl.ds(0, 12)],
                key_in.at[z, pl.ds(0, 12)],
                keys_sent,
                keys_sem,
                at(zl_=line, zh_=half),
            ).start()

        if h == 1:
            send(1 - zh, zl)
        for k in (4, 3, 5, 2, 6, 1, 7):
            send(h, lax.rem(zl + k, 8))

    def finish():
        key_in[z] = key_part[zh, zl]
        keys_here.wait_recv()
        total = key_in[0, 0:12]
        for k in range(1, 16):
            total = total + key_in[k, 0:12]
        keys_out[...] = jnp.zeros_like(keys_out)
        keys_out[0:12, :] = total
        keys = keys_out[...].astype(BF16)

        new = (
            lax.dot_general(
                q32[...].astype(BF16), keys, (((1,), (1,)), ((), ())), preferred_element_type=F32
            )
            * scale
        )
        row = lax.broadcasted_iota(jnp.int32, (128, 16), 0)
        column = lax.broadcasted_iota(jnp.int32, (128, 16), 1)
        same_row = (row // 32) == (column % 4)
        earlier = (column // 4) <= ((row % 32) // 8)
        new = jnp.where(same_row & earlier & (column < 12), new, -jnp.inf)
        top = jnp.maximum(old_top[...], jnp.max(new, axis=1, keepdims=True))
        fade = jnp.exp(old_top[...] - top)
        new = jnp.exp(new - top)
        total = old_sum[...] * fade + jnp.sum(new, axis=1, keepdims=True)
        new_probs = (new / total).astype(BF16)
        share = fade / total
        attended = jnp.dot(new_probs, sv32[...].astype(BF16), preferred_element_type=F32)
        for r in range(4):
            rows = slice(32 * r, 32 * r + 32)
            probs = (old_exp[rows, :] * share[rows]).astype(BF16)
            att = attended[rows] + jnp.dot(probs, cv_v[r, 0], preferred_element_type=F32)
            for s in range(3):
                att_out[s, r] = att[8 * s : 8 * s + 8]

    def adam_loads():
        adam_load.wait()

    schedule = (
        (local_term, 0),
        (hop, 1),
        (local_term, 1),
        (hop, 2),
        (ring_first, 0),
        (local_term, 2),
        (hop, 3),
        (ring_first, 1),
        (local_term, 3),
        (hop, 4),
        (ring_second, 0),
        (ring_first, 2),
        (hop, 5),
        (ring_second, 1),
        (line_pair, 0),
        (ring_first, 3),
        (hop, 6),
        (ring_second, 2),
        (line_pair, 1),
        (hop, 7),
        (line_quad, 0),
        (ring_second, 3),
        (line_pair, 2),
        (line_quad, 1),
        (line_pair, 3),
        (line_quad, 2),
        (line_quad, 3),
        (send_rows,),
        (adam_loads,),
        (update, 0),
        (update, 1),
        (head_columns, 0),
        (update, 2),
        (share_weights, 0),
        (update, 3),
        (head_columns, 1),
        (make_normed,),
        (send_keys, 0),
        (old_scores,),
        (share_weights, 1),
        (send_keys, 1),
        (finish,),
    )
    for do, *chunk in schedule:
        do(*chunk)

    for copy in sent:
        copy.wait_send()
    assert sems.used == N_SEMS, sems.used


def store(
    master_v, one_v, two_v, keys_v, att_v, step_v, master, one, two, keys, decoded, keys_b, dec_b, sems
):
    copies = []

    def start(src, dst):
        copies.append(pltpu.make_async_copy(src, dst, sems.at[len(copies)]))
        copies[-1].start()

    start(master_v, master)
    start(one_v, one)
    start(two_v, two)
    for s in range(3):
        keys_b[s] = keys_v[4 * s : 4 * s + 4, :].astype(BF16)
    start(keys_b, keys)
    for s in range(3):
        for g in range(8):
            columns = slice(128 * g, 128 * g + 128)
            dec_b[s, :, columns] = (
                step_v[s, :, columns].astype(F32) + att_v[s, :, g, :]
            ).astype(BF16)
    start(dec_b, decoded)
    for copy in copies:
        copy.wait()


def body(
    train_inputs,
    key_cotangent,
    master,
    moment_one,
    moment_two,
    step_inputs,
    decode_queries,
    step_values,
    cache_keys,
    cache_values,
    cache_lengths,
    norm_gain,
):
    hbm = pl.BlockSpec(memory_space=pltpu.HBM)
    vmem = pl.BlockSpec(memory_space=pltpu.VMEM)
    owned = jax.ShapeDtypeStruct(master.shape, F32)
    owned_v = pltpu.VMEM(master.shape, F32)
    results = pl.pallas_call(
        kernel,
        out_shape=(
            owned_v,
            owned_v,
            owned_v,
            pltpu.VMEM((16, 128), F32),
            pltpu.VMEM((3, 4, 8, 128), F32),
        ),
        in_specs=[hbm] * 10 + [pl.BlockSpec(memory_space=pltpu.SMEM), hbm],
        out_specs=(vmem,) * 5,
        scratch_shapes=[
            pltpu.VMEM((1024, 1024), BF16),
            pltpu.VMEM((1024, 1024), BF16),
            pltpu.VMEM((3, 1, 16, 1024), F32),
            pltpu.VMEM((3, 4, 1024), BF16),
            pltpu.VMEM((3, 4, 8, 128), BF16),
            pltpu.VMEM((3, 4, 128), BF16),
            pltpu.VMEM((4, 1, 512, 128), BF16),
            pltpu.VMEM((4, 1, 512, 128), BF16),
            pltpu.VMEM((64, 128), F32),
            pltpu.VMEM((CHUNKS, 2, 8, 4, 16, CW), F32),
            pltpu.VMEM((CHUNKS, 8, 4, 16, CW), F32),
            pltpu.VMEM((CHUNKS, 6, 4, 16, CW), BF16),
            pltpu.VMEM((CHUNKS, 6, 4, 16, CW), BF16),
            pltpu.VMEM((CHUNKS, 8, 16, CW), F32),
            pltpu.VMEM((CHUNKS, 4, 16, CW), BF16),
            pltpu.VMEM((CHUNKS, 4, 16, CW), BF16),
            pltpu.VMEM((CHUNKS, 4, 16, CW), F32),
            pltpu.VMEM((CHUNKS, 4, 16, CW), BF16),
            pltpu.VMEM((CHUNKS, 3, 16, CW), BF16),
            pltpu.VMEM((16, 1024), F32),
            pltpu.VMEM((4, 8, 16, 128), BF16),
            pltpu.VMEM((8, 4, 16, 128), BF16),
            pltpu.VMEM((16, 1, 128), F32),
            pltpu.VMEM((128, 512), BF16),
            pltpu.VMEM((2, 4, 16, 128), BF16),
            pltpu.VMEM((2, 4, 4, 2, 16, 128), BF16),
            pltpu.VMEM((2, 8, 16, 128), F32),
            pltpu.VMEM((16, 16, 128), F32),
            pltpu.VMEM((128, 128), F32),
            pltpu.VMEM((128, 512), F32),
            pltpu.VMEM((128, 1), F32),
            pltpu.VMEM((128, 1), F32),
            pltpu.VMEM((16, 128), F32),
            pltpu.SemaphoreType.DMA((N_SEMS,)),
            pltpu.SemaphoreType.REGULAR((7,)),
        ],
        compiler_params=pltpu.CompilerParams(
            collective_id=0, has_side_effects=True, vmem_limit_bytes=40 << 20
        ),
        name="adam_decode",
    )(
        *(
            pltpu.with_memory_space_constraint(array, pltpu.HBM)
            for array in (
                train_inputs,
                key_cotangent,
                master,
                moment_one,
                moment_two,
                step_inputs,
                decode_queries,
                step_values.reshape(3, 4, 128),
                cache_keys,
                cache_values,
            )
        ),
        cache_lengths,
        pltpu.with_memory_space_constraint(norm_gain.reshape(64, 128), pltpu.HBM),
    )
    new_master, new_one, new_two, new_keys, decoded = pl.pallas_call(
        store,
        out_shape=(
            owned,
            owned,
            owned,
            jax.ShapeDtypeStruct((3, 4, 128), BF16),
            jax.ShapeDtypeStruct(step_inputs.shape, BF16),
        ),
        in_specs=[vmem] * 6,
        out_specs=(hbm,) * 5,
        scratch_shapes=[
            pltpu.VMEM((3, 4, 128), BF16),
            pltpu.VMEM((3, 4, 1024), BF16),
            pltpu.SemaphoreType.DMA((5,)),
        ],
        compiler_params=pltpu.CompilerParams(vmem_limit_bytes=40 << 20),
        name="store_results",
    )(*results, step_inputs)
    return new_master, new_one, new_two, new_keys.reshape(step_values.shape), decoded


def solution(mesh):
    return jax.shard_map(
        body,
        mesh=mesh,
        in_specs=(
            P("fsdp", "tp"),
            P("fsdp", None),
            P("tp", "fsdp", None),
            P("tp", "fsdp", None),
            P("tp", "fsdp", None),
            P(None, "fsdp", "tp"),
            P(None, "fsdp", "tp", None),
            P(None, "fsdp", "tp", None),
            P("fsdp", "tp", None, None),
            P("fsdp", "tp", None, None),
            P("fsdp"),
            P(),
        ),
        out_specs=(
            P("tp", "fsdp", None),
            P("tp", "fsdp", None),
            P("tp", "fsdp", None),
            P(None, "fsdp", "tp", None),
            P(None, "fsdp", "tp"),
        ),
        check_vma=False,
    )
```

```python
import functools

import jax
import jax.numpy as jnp
from jax import lax
from jax.experimental import pallas as pl
from jax.experimental.pallas import tpu as pltpu
from jax.sharding import PartitionSpec as P

MESH = pl.DeviceIdType.MESH
correction_one = 1.0 - 0.9**4
correction_two = 1.0 - 0.95**4

CHUNKS = 4
CW = 1024 // CHUNKS
F32 = jnp.float32
BF16 = jnp.bfloat16


class Sems:
    def __init__(self, sems):
        self.sems, self.used = sems, 0

    def new(self):
        self.used += 1
        return self.sems.at[self.used - 1]


def remote(src, dst, send_sem, recv_sem, device):
    return pltpu.make_async_remote_copy(
        src_ref=src,
        dst_ref=dst,
        send_sem=send_sem,
        recv_sem=recv_sem,
        device_id=device,
        device_id_type=MESH,
    )


N_SEMS = 25 + 7 * CHUNKS


def kernel(
    x_hbm,
    c_hbm,
    master_hbm,
    one_hbm,
    two_hbm,
    step_hbm,
    query_hbm,
    value_hbm,
    ck_hbm,
    cv_hbm,
    lengths_hbm,
    gain_hbm,
    new_master,
    new_one,
    new_two,
    keys_out,
    att_out,
    x_v,
    c_v,
    adam_v,
    step_v,
    query_v,
    value_v,
    ck_v,
    cv_v,
    gain_v,
    lengths,
    part,
    part_out,
    part_in,
    ring_out,
    ring_in,
    line_sum,
    pair_out,
    pair_in,
    quad_sum,
    quad_out,
    quad_in,
    rows32,
    rows_y,
    rows_z,
    squares,
    normed,
    w_out,
    w_all,
    key_part,
    key_in,
    q32,
    old_exp,
    old_top,
    old_sum,
    sv32,
    copy_sems,
    far_sems,
):
    f, t = lax.axis_index("fsdp"), lax.axis_index("tp")
    core = lax.rem(f, 2)
    x = lax.rem(lax.div(f, 2), 4)
    zl = lax.div(f, 8)
    y = lax.rem(t, 4)
    zh = lax.div(t, 4)
    z = zh * 8 + zl

    def fsdp(zl_, x_, core_):
        return (zl_ * 4 + x_) * 2 + core_

    def at(zl_=zl, x_=x, core_=core, zh_=zh, y_=y):
        return {"fsdp": fsdp(zl_, x_, core_), "tp": zh_ * 4 + y_}

    sibling = at(core_=1 - core)
    x_peer = [None] + [at(x_=lax.rem(x + k, 4)) for k in (1, 2, 3)]
    y_peer = [None] + [at(y_=lax.rem(y + k, 4)) for k in (1, 2, 3)]

    def z_of(k):
        return lax.rem(z + k, 16)

    def z_peer(k):
        other = z_of(k)
        return at(zl_=lax.rem(other, 8), zh_=lax.div(other, 8))

    sems = Sems(copy_sems)

    barrier = pltpu.get_barrier_semaphore()
    places = [
        (kx, ky, kc) for kx in (2, 1, 3, 0) for ky in (2, 1, 3, 0) for kc in (0, 1)
    ]
    places.remove((0, 0, 0))
    plane = [
        at(x_=lax.rem(x + kx, 4), y_=lax.rem(y + ky, 4), core_=1 - core if kc else core)
        for kx, ky, kc in places
    ]
    partners = plane + [z_peer(1), z_peer(15)]
    for partner in partners:
        pl.semaphore_signal(barrier, inc=1, device_id=partner, device_id_type=MESH)

    def load(pairs, whole=None):
        sem = sems.new()
        for src, dst in pairs:
            pltpu.make_async_copy(src, dst, sem).start()
        return pltpu.make_async_copy(*(whole or pairs[0]), sem)

    step_load = load([(step_hbm, step_v)])
    x_load = load([(x_hbm, x_v)])
    c_loads = []
    for j in range(CHUNKS):
        columns = slice(j * CW, (j + 1) * CW)
        c_loads.append(load([(c_hbm.at[:, columns], c_v.at[:, columns])]))
    score_loads = [
        load([pair])
        for pair in (
            (query_hbm, query_v),
            (ck_hbm, ck_v),
            (cv_hbm, cv_v),
            (value_hbm, value_v),
            (lengths_hbm, lengths),
        )
    ]
    gain_load = load([(gain_hbm, gain_v)])
    adam_load = load(
        [(ref, adam_v.at[k]) for k, ref in enumerate((master_hbm, one_hbm, two_hbm))],
        (adam_v, adam_v),
    )

    step_load.wait()
    rows32[...] = jnp.zeros_like(rows32)
    for s in range(3):
        rows32[4 * s : 4 * s + 4, :] = step_v[s].astype(F32)
    for k in range(8):
        rows_y[y, k] = rows32[:, 128 * k : 128 * k + 128].astype(BF16)

    pl.semaphore_wait(barrier, len(partners))
    sent = []

    def sender(whole):
        sem = sems.new()
        sent.append(remote(whole, whole, sem, sem, sibling))
        return sem

    def arrival(whole):
        sem = sems.new()
        return sem, remote(whole, whole, sem, sem, sibling)

    def hop(d):
        if d > 0:
            pl.semaphore_wait(far_sems.at[d - 1], 2)
        if d < 7:
            for partner in (z_peer(1), z_peer(15)):
                pl.semaphore_signal(
                    far_sems.at[d], inc=1, device_id=partner, device_id_type=MESH
                )

    hop(0)
    own_sent, (own_sem, own_rows) = sender(rows_y.at[0:3]), arrival(rows_y.at[0:3])
    for k in (2, 1, 3):
        remote(rows_y.at[y], rows_y.at[y], own_sent, own_sem, y_peer[k]).start()

    swap_sent = sender(part_out)
    swaps = [arrival(part_in.at[j]) for j in range(CHUNKS)]

    def local_term(j):
        if j == 0:
            x_load.wait()
        c_loads[j].wait()
        term = lax.dot_general(
            x_v[...],
            c_v[:, j * CW : (j + 1) * CW],
            (((0,), (0,)), ((), ())),
            preferred_element_type=F32,
        ).reshape(8, 4, 2, 16, CW)
        part[j, 0] = term[:, :, 0]
        part[j, 1] = term[:, :, 1]
        part_out[j] = part[j, 1 - core].astype(BF16)
        remote(part_out.at[j], part_in.at[j], swap_sent, swaps[j][0], sibling).start()

    xp, xo, xm = (lax.rem(x + k, 4) for k in (1, 2, 3))
    low, high = slice(0, 4), slice(4, 8)
    ring_sent = sender(ring_out)
    ring = [
        [arrival(ring_in.at[j, 0]), arrival(ring_in.at[j, 1])]
        + [arrival(ring_in.at[j, 2:6])] * 4
        for j in range(CHUNKS)
    ]
    pair_sent = sender(pair_out)
    pairs = [arrival(pair_in.at[j]) for j in range(CHUNKS)]
    quad_sent = sender(quad_out.at[:, 0:3])
    quads = [arrival(quad_in.at[j]) for j in range(CHUNKS)]
    parity, quad = lax.rem(zl, 2), lax.div(zl, 2)

    def chip_sum(j, half, target):
        return part[j, core, half, target] + part_in[j, half, target].astype(F32)

    def ring_send(j, number, value, device):
        ring_out[j, number] = value.astype(BF16)
        remote(
            ring_out.at[j, number], ring_in.at[j, number], ring_sent, ring[j][number][0], device
        ).start()

    def ring_first(j):
        swaps[j][1].wait_recv()
        ring_send(j, 0, chip_sum(j, low, xo), x_peer[1])
        ring_send(j, 1, chip_sum(j, high, xo), x_peer[3])
        ring_send(j, 2, chip_sum(j, high, xp), x_peer[1])
        ring_send(j, 3, chip_sum(j, low, xm), x_peer[3])

    def ring_second(j):
        ring[j][0][1].wait_recv()
        ring_send(j, 4, chip_sum(j, low, xp) + ring_in[j, 0].astype(F32), x_peer[1])
        ring[j][1][1].wait_recv()
        ring_send(j, 5, chip_sum(j, high, xm) + ring_in[j, 1].astype(F32), x_peer[3])

    def line_pair(j):
        ring[j][2][1].wait_recv()
        line_sum[j, low] = (
            chip_sum(j, low, x) + ring_in[j, 3].astype(F32) + ring_in[j, 4].astype(F32)
        )
        line_sum[j, high] = (
            chip_sum(j, high, x) + ring_in[j, 2].astype(F32) + ring_in[j, 5].astype(F32)
        )
        for q in range(4):
            pair_out[j, q] = line_sum[j, 2 * q + 1 - parity].astype(BF16)
        remote(
            pair_out.at[j], pair_in.at[j], pair_sent, pairs[j][0], at(zl_=zl + 1 - 2 * parity)
        ).start()

    def line_quad(j):
        pairs[j][1].wait_recv()
        for q in range(4):
            total = line_sum[j, 2 * q + parity] + pair_in[j, q].astype(F32)
            quad_sum[j, q] = total
            quad_out[j, q] = total.astype(BF16)
        for k in (2, 3, 1):
            other = lax.rem(quad + k, 4)
            remote(
                quad_out.at[j, other],
                quad_in.at[j, k - 1],
                quad_sent,
                quads[j][0],
                at(zl_=2 * other + parity),
            ).start()

    def update(j):
        quads[j][1].wait_recv()
        gradient = quad_sum[j, quad]
        for k in (1, 2, 3):
            gradient = gradient + quad_in[j, k - 1].astype(F32)
        columns = slice(j * CW, (j + 1) * CW)
        one = 0.9 * adam_v[1, 0, :, columns] + 0.1 * gradient
        two = 0.95 * adam_v[2, 0, :, columns] + 0.05 * gradient * gradient
        fresh = adam_v[0, 0, :, columns] - 0.003 * (one / correction_one) / (
            jnp.sqrt(two / correction_two) + 1e-08
        )
        new_one[0, :, columns] = one
        new_two[0, :, columns] = two
        new_master[0, :, columns] = fresh
        weights = fresh.astype(BF16)
        for k in range(CW // 128):
            head = j * (CW // 128) + k
            w_out[head // 4, head % 4] = weights[:, 128 * k : 128 * k + 128]

    lane = lax.broadcasted_iota(jnp.int32, (16, 128), 1)
    diagonal = lane == lax.broadcasted_iota(jnp.int32, (16, 128), 0)
    rows_sent, (rows_sem, rows_here) = sender(rows_z.at[0:7]), arrival(rows_z.at[0:7])
    squares_sent, (squares_sem, squares_here) = (
        sender(squares.at[0:15]),
        arrival(squares.at[0:15]),
    )

    def send_rows():
        own_rows.wait_recv()
        for k in (4, 3, 5, 2, 6, 1, 7):
            other = lax.rem(zl + k, 8)
            remote(
                rows_y.at[:, other], rows_z.at[zl], rows_sent, rows_sem, at(zl_=other)
            ).start()
        total = jnp.zeros((16, 128), F32)
        for q in range(4):
            for k in range(8):
                block = rows_y[q, k].astype(F32)
                total = total + block * block
        column = jnp.sum(total, axis=1, keepdims=True)
        squares[z] = jnp.sum(jnp.where(diagonal, column, 0.0), axis=0, keepdims=True)
        for k in (8, 7, 9, 6, 10, 5, 11, 4, 12, 3, 13, 2, 14, 1, 15):
            remote(squares.at[z], squares.at[z], squares_sent, squares_sem, z_peer(k)).start()
        for q in range(4):
            rows_z[zl, q] = rows_y[q, zl]

    def make_normed():
        gain_load.wait()
        squares_here.wait_recv()
        rows_here.wait_recv()
        for s in range(8):
            both = squares[s] + squares[s + 8]
            column = jnp.sum(jnp.where(diagonal, both, 0.0), axis=1, keepdims=True)
            inverse = lax.rsqrt(column * (1.0 / 8192.0) + 1e-06)
            for q in range(4):
                gain = gain_v[pl.ds((zh * 4 + q) * 8 + zl, 1), :]
                block = rows_z[s, q].astype(F32) * inverse * gain
                normed[16 * s : 16 * s + 16, 128 * q : 128 * q + 128] = block.astype(BF16)

    scale = 1.0 / 128.0**0.5

    def old_scores():
        for copy in score_loads:
            copy.wait()
        q32[...] = jnp.zeros_like(q32)
        for s in range(3):
            for r in range(4):
                q32[32 * r + 8 * s : 32 * r + 8 * s + 8, :] = query_v[s, r].astype(F32)
        sv32[...] = jnp.zeros_like(sv32)
        for s in range(3):
            sv32[4 * s : 4 * s + 4, :] = value_v[s].astype(F32)
        slot = lax.broadcasted_iota(jnp.int32, (32, 512), 1)
        for r in range(4):
            scores = (
                lax.dot_general(
                    q32[32 * r : 32 * r + 32, :].astype(BF16),
                    ck_v[r, 0],
                    (((1,), (1,)), ((), ())),
                    preferred_element_type=F32,
                )
                * scale
            )
            scores = jnp.where(slot < lengths[r], scores, -jnp.inf)
            top = jnp.max(scores, axis=1, keepdims=True)
            weight = jnp.exp(scores - top)
            rows = slice(32 * r, 32 * r + 32)
            old_exp[rows, :] = weight
            old_top[rows, :] = top
            old_sum[rows, :] = jnp.sum(weight, axis=1, keepdims=True)

    shared_sent = [sender(w_all.at[0, 0:31]) for h in range(2)]
    shared = [arrival(w_all.at[0, 0:31]) for h in range(2)]
    keys_sent = sender(key_in.at[0:15, pl.ds(0, 12)])
    keys_sem, keys_here = arrival(key_in.at[0:15, pl.ds(0, 12)])

    def head_columns(h):
        slot = (y * 4 + x) * 2 + core
        for (_, ky, _), device in zip(places, plane):
            remote(
                w_out.at[h, lax.rem(y + ky, 4)],
                w_all.at[h, slot],
                shared_sent[h],
                shared[h][0],
                device,
            ).start()
        w_all[h, slot] = w_out[h, y]

    def send_keys(h):
        shared[h][1].wait_recv()
        key_part[h] = jnp.dot(
            normed[...], w_all[h].reshape(512, 128), preferred_element_type=F32
        ).reshape(8, 16, 128)

        def send(half, line):
            remote(
                key_part.at[half, line, pl.ds(0, 12)],
                key_in.at[z, pl.ds(0, 12)],
                keys_sent,
                keys_sem,
                at(zl_=line, zh_=half),
            ).start()

        if h == 1:
            send(1 - zh, zl)
        for k in (4, 3, 5, 2, 6, 1, 7):
            send(h, lax.rem(zl + k, 8))

    def finish():
        key_in[z] = key_part[zh, zl]
        keys_here.wait_recv()
        total = key_in[0, 0:12]
        for k in range(1, 16):
            total = total + key_in[k, 0:12]
        keys_out[...] = jnp.zeros_like(keys_out)
        keys_out[0:12, :] = total
        keys = keys_out[...].astype(BF16)

        new = (
            lax.dot_general(
                q32[...].astype(BF16), keys, (((1,), (1,)), ((), ())), preferred_element_type=F32
            )
            * scale
        )
        row = lax.broadcasted_iota(jnp.int32, (128, 16), 0)
        column = lax.broadcasted_iota(jnp.int32, (128, 16), 1)
        same_row = (row // 32) == (column % 4)
        earlier = (column // 4) <= ((row % 32) // 8)
        new = jnp.where(same_row & earlier & (column < 12), new, -jnp.inf)
        top = jnp.maximum(old_top[...], jnp.max(new, axis=1, keepdims=True))
        fade = jnp.exp(old_top[...] - top)
        new = jnp.exp(new - top)
        total = old_sum[...] * fade + jnp.sum(new, axis=1, keepdims=True)
        new_probs = (new / total).astype(BF16)
        share = fade / total
        attended = jnp.dot(new_probs, sv32[...].astype(BF16), preferred_element_type=F32)
        for r in range(4):
            rows = slice(32 * r, 32 * r + 32)
            probs = (old_exp[rows, :] * share[rows]).astype(BF16)
            att = attended[rows] + jnp.dot(probs, cv_v[r, 0], preferred_element_type=F32)
            for s in range(3):
                att_out[s, r] = att[8 * s : 8 * s + 8]

    def adam_loads():
        adam_load.wait()

    schedule = (
        (local_term, 0),
        (hop, 1),
        (local_term, 1),
        (ring_first, 0),
        (hop, 2),
        (local_term, 2),
        (ring_first, 1),
        (hop, 3),
        (local_term, 3),
        (ring_second, 0),
        (hop, 4),
        (ring_first, 2),
        (ring_second, 1),
        (hop, 5),
        (line_pair, 0),
        (ring_first, 3),
        (hop, 6),
        (ring_second, 2),
        (line_pair, 1),
        (hop, 7),
        (line_quad, 0),
        (ring_second, 3),
        (line_pair, 2),
        (line_quad, 1),
        (line_pair, 3),
        (line_quad, 2),
        (line_quad, 3),
        (send_rows,),
        (adam_loads,),
        (update, 0),
        (update, 1),
        (head_columns, 0),
        (update, 2),
        (update, 3),
        (head_columns, 1),
        (old_scores,),
        (make_normed,),
        (send_keys, 0),
        (send_keys, 1),
        (finish,),
    )
    for do, *chunk in schedule:
        do(*chunk)

    for copy in sent:
        copy.wait_send()
    assert sems.used == N_SEMS, sems.used


def store(
    master_v, one_v, two_v, keys_v, att_v, step_v, master, one, two, keys, decoded, keys_b, dec_b, sems
):
    copies = []

    def start(src, dst):
        copies.append(pltpu.make_async_copy(src, dst, sems.at[len(copies)]))
        copies[-1].start()

    start(master_v, master)
    start(one_v, one)
    start(two_v, two)
    for s in range(3):
        keys_b[s] = keys_v[4 * s : 4 * s + 4, :].astype(BF16)
    start(keys_b, keys)
    for s in range(3):
        for g in range(8):
            columns = slice(128 * g, 128 * g + 128)
            dec_b[s, :, columns] = (
                step_v[s, :, columns].astype(F32) + att_v[s, :, g, :]
            ).astype(BF16)
    start(dec_b, decoded)
    for copy in copies:
        copy.wait()


def body(
    train_inputs,
    key_cotangent,
    master,
    moment_one,
    moment_two,
    step_inputs,
    decode_queries,
    step_values,
    cache_keys,
    cache_values,
    cache_lengths,
    norm_gain,
):
    hbm = pl.BlockSpec(memory_space=pltpu.HBM)
    vmem = pl.BlockSpec(memory_space=pltpu.VMEM)
    owned = jax.ShapeDtypeStruct(master.shape, F32)
    owned_v = pltpu.VMEM(master.shape, F32)
    results = pl.pallas_call(
        kernel,
        out_shape=(
            owned_v,
            owned_v,
            owned_v,
            pltpu.VMEM((16, 128), F32),
            pltpu.VMEM((3, 4, 8, 128), F32),
        ),
        in_specs=[hbm] * 12,
        out_specs=(vmem,) * 5,
        scratch_shapes=[
            pltpu.VMEM((1024, 1024), BF16),
            pltpu.VMEM((1024, 1024), BF16),
            pltpu.VMEM((3, 1, 16, 1024), F32),
            pltpu.VMEM((3, 4, 1024), BF16),
            pltpu.VMEM((3, 4, 8, 128), BF16),
            pltpu.VMEM((3, 4, 128), BF16),
            pltpu.VMEM((4, 1, 512, 128), BF16),
            pltpu.VMEM((4, 1, 512, 128), BF16),
            pltpu.VMEM((64, 128), F32),
            pltpu.SMEM((4,), jnp.int32),
            pltpu.VMEM((CHUNKS, 2, 8, 4, 16, CW), F32),
            pltpu.VMEM((CHUNKS, 8, 4, 16, CW), BF16),
            pltpu.VMEM((CHUNKS, 8, 4, 16, CW), BF16),
            pltpu.VMEM((CHUNKS, 6, 4, 16, CW), BF16),
            pltpu.VMEM((CHUNKS, 6, 4, 16, CW), BF16),
            pltpu.VMEM((CHUNKS, 8, 16, CW), F32),
            pltpu.VMEM((CHUNKS, 4, 16, CW), BF16),
            pltpu.VMEM((CHUNKS, 4, 16, CW), BF16),
            pltpu.VMEM((CHUNKS, 4, 16, CW), F32),
            pltpu.VMEM((CHUNKS, 4, 16, CW), BF16),
            pltpu.VMEM((CHUNKS, 3, 16, CW), BF16),
            pltpu.VMEM((16, 1024), F32),
            pltpu.VMEM((4, 8, 16, 128), BF16),
            pltpu.VMEM((8, 4, 16, 128), BF16),
            pltpu.VMEM((16, 1, 128), F32),
            pltpu.VMEM((128, 512), BF16),
            pltpu.VMEM((2, 4, 16, 128), BF16),
            pltpu.VMEM((2, 32, 16, 128), BF16),
            pltpu.VMEM((2, 8, 16, 128), F32),
            pltpu.VMEM((16, 16, 128), F32),
            pltpu.VMEM((128, 128), F32),
            pltpu.VMEM((128, 512), F32),
            pltpu.VMEM((128, 1), F32),
            pltpu.VMEM((128, 1), F32),
            pltpu.VMEM((16, 128), F32),
            pltpu.SemaphoreType.DMA((N_SEMS,)),
            pltpu.SemaphoreType.REGULAR((7,)),
        ],
        compiler_params=pltpu.CompilerParams(
            collective_id=0, has_side_effects=True, vmem_limit_bytes=40 << 20
        ),
        name="adam_decode",
    )(
        *(
            pltpu.with_memory_space_constraint(array, pltpu.HBM)
            for array in (
                train_inputs,
                key_cotangent,
                master,
                moment_one,
                moment_two,
                step_inputs,
                decode_queries,
                step_values.reshape(3, 4, 128),
                cache_keys,
                cache_values,
                cache_lengths,
                norm_gain.reshape(64, 128),
            )
        ),
    )
    new_master, new_one, new_two, new_keys, decoded = pl.pallas_call(
        store,
        out_shape=(
            owned,
            owned,
            owned,
            jax.ShapeDtypeStruct((3, 4, 128), BF16),
            jax.ShapeDtypeStruct(step_inputs.shape, BF16),
        ),
        in_specs=[vmem] * 6,
        out_specs=(hbm,) * 5,
        scratch_shapes=[
            pltpu.VMEM((3, 4, 128), BF16),
            pltpu.VMEM((3, 4, 1024), BF16),
            pltpu.SemaphoreType.DMA((5,)),
        ],
        compiler_params=pltpu.CompilerParams(vmem_limit_bytes=40 << 20),
        name="store_results",
    )(*results, step_inputs)
    return new_master, new_one, new_two, new_keys.reshape(step_values.shape), decoded


def solution(mesh):
    return jax.shard_map(
        body,
        mesh=mesh,
        in_specs=(
            P("fsdp", "tp"),
            P("fsdp", None),
            P("tp", "fsdp", None),
            P("tp", "fsdp", None),
            P("tp", "fsdp", None),
            P(None, "fsdp", "tp"),
            P(None, "fsdp", "tp", None),
            P(None, "fsdp", "tp", None),
            P("fsdp", "tp", None, None),
            P("fsdp", "tp", None, None),
            P("fsdp"),
            P(),
        ),
        out_specs=(
            P("tp", "fsdp", None),
            P("tp", "fsdp", None),
            P("tp", "fsdp", None),
            P(None, "fsdp", "tp", None),
            P(None, "fsdp", "tp"),
        ),
        check_vma=False,
    )
```

```python
import functools

import jax
import jax.numpy as jnp
from jax import lax
from jax.experimental import pallas as pl
from jax.experimental.pallas import tpu as pltpu
from jax.sharding import PartitionSpec as P

MESH = pl.DeviceIdType.MESH
correction_one = 1.0 - 0.9**4
correction_two = 1.0 - 0.95**4

CHUNKS = 4
CW = 1024 // CHUNKS
F32 = jnp.float32
BF16 = jnp.bfloat16


class Sems:
    def __init__(self, sems):
        self.sems, self.used = sems, 0

    def new(self):
        self.used += 1
        return self.sems.at[self.used - 1]


def remote(src, dst, send_sem, recv_sem, device):
    return pltpu.make_async_remote_copy(
        src_ref=src,
        dst_ref=dst,
        send_sem=send_sem,
        recv_sem=recv_sem,
        device_id=device,
        device_id_type=MESH,
    )


N_SEMS = 25 + 7 * CHUNKS


def kernel(
    x_hbm,
    c_hbm,
    master_hbm,
    one_hbm,
    two_hbm,
    step_hbm,
    query_hbm,
    value_hbm,
    ck_hbm,
    cv_hbm,
    lengths_hbm,
    gain_hbm,
    new_master,
    new_one,
    new_two,
    keys_out,
    att_out,
    x_v,
    c_v,
    adam_v,
    step_v,
    query_v,
    value_v,
    ck_v,
    cv_v,
    gain_v,
    lengths,
    part,
    part_out,
    part_in,
    ring_out,
    ring_in,
    line_sum,
    pair_out,
    pair_in,
    quad_sum,
    quad_out,
    quad_in,
    rows32,
    rows_y,
    rows_z,
    squares,
    normed,
    w_out,
    w_all,
    key_part,
    key_in,
    q32,
    old_exp,
    old_top,
    old_sum,
    sv32,
    copy_sems,
    far_sems,
):
    f, t = lax.axis_index("fsdp"), lax.axis_index("tp")
    core = lax.rem(f, 2)
    x = lax.rem(lax.div(f, 2), 4)
    zl = lax.div(f, 8)
    y = lax.rem(t, 4)
    zh = lax.div(t, 4)
    z = zh * 8 + zl

    def fsdp(zl_, x_, core_):
        return (zl_ * 4 + x_) * 2 + core_

    def at(zl_=zl, x_=x, core_=core, zh_=zh, y_=y):
        return {"fsdp": fsdp(zl_, x_, core_), "tp": zh_ * 4 + y_}

    sibling = at(core_=1 - core)
    x_peer = [None] + [at(x_=lax.rem(x + k, 4)) for k in (1, 2, 3)]
    y_peer = [None] + [at(y_=lax.rem(y + k, 4)) for k in (1, 2, 3)]

    def z_of(k):
        return lax.rem(z + k, 16)

    def z_peer(k):
        other = z_of(k)
        return at(zl_=lax.rem(other, 8), zh_=lax.div(other, 8))

    sems = Sems(copy_sems)

    barrier = pltpu.get_barrier_semaphore()
    places = [
        (kx, ky, kc) for kx in (2, 1, 3, 0) for ky in (2, 1, 3, 0) for kc in (0, 1)
    ]
    places.remove((0, 0, 0))
    plane = [
        at(x_=lax.rem(x + kx, 4), y_=lax.rem(y + ky, 4), core_=1 - core if kc else core)
        for kx, ky, kc in places
    ]
    partners = plane + [z_peer(1), z_peer(15)]
    for partner in partners:
        pl.semaphore_signal(barrier, inc=1, device_id=partner, device_id_type=MESH)

    def load(pairs, whole=None):
        sem = sems.new()
        for src, dst in pairs:
            pltpu.make_async_copy(src, dst, sem).start()
        return pltpu.make_async_copy(*(whole or pairs[0]), sem)

    step_load = load([(step_hbm, step_v)])
    x_load = load([(x_hbm, x_v)])
    c_loads = []
    for j in range(CHUNKS):
        columns = slice(j * CW, (j + 1) * CW)
        c_loads.append(load([(c_hbm.at[:, columns], c_v.at[:, columns])]))
    score_loads = [
        load([pair])
        for pair in (
            (query_hbm, query_v),
            (ck_hbm, ck_v),
            (cv_hbm, cv_v),
            (value_hbm, value_v),
            (lengths_hbm, lengths),
        )
    ]
    gain_load = load([(gain_hbm, gain_v)])
    adam_load = load(
        [(ref, adam_v.at[k]) for k, ref in enumerate((master_hbm, one_hbm, two_hbm))],
        (adam_v, adam_v),
    )

    step_load.wait()
    rows32[...] = jnp.zeros_like(rows32)
    for s in range(3):
        rows32[4 * s : 4 * s + 4, :] = step_v[s].astype(F32)
    for k in range(8):
        rows_y[y, k] = rows32[:, 128 * k : 128 * k + 128].astype(BF16)

    pl.semaphore_wait(barrier, len(partners))
    sent = []

    def sender(whole):
        sem = sems.new()
        sent.append(remote(whole, whole, sem, sem, sibling))
        return sem

    def arrival(whole):
        sem = sems.new()
        return sem, remote(whole, whole, sem, sem, sibling)

    def hop(d):
        if d > 0:
            pl.semaphore_wait(far_sems.at[d - 1], 2)
        if d < 7:
            for partner in (z_peer(1), z_peer(15)):
                pl.semaphore_signal(
                    far_sems.at[d], inc=1, device_id=partner, device_id_type=MESH
                )

    hop(0)
    own_sent, (own_sem, own_rows) = sender(rows_y.at[0:3]), arrival(rows_y.at[0:3])
    for k in (2, 1, 3):
        remote(rows_y.at[y], rows_y.at[y], own_sent, own_sem, y_peer[k]).start()

    swap_sent = sender(part_out)
    swaps = [arrival(part_in.at[j]) for j in range(CHUNKS)]

    def local_term(j):
        if j == 0:
            x_load.wait()
        c_loads[j].wait()
        term = lax.dot_general(
            x_v[...],
            c_v[:, j * CW : (j + 1) * CW],
            (((0,), (0,)), ((), ())),
            preferred_element_type=F32,
        ).reshape(8, 4, 2, 16, CW)
        part[j, 0] = term[:, :, 0]
        part[j, 1] = term[:, :, 1]
        part_out[j] = part[j, 1 - core].astype(BF16)
        remote(part_out.at[j], part_in.at[j], swap_sent, swaps[j][0], sibling).start()

    xp, xo, xm = (lax.rem(x + k, 4) for k in (1, 2, 3))
    low, high = slice(0, 4), slice(4, 8)
    ring_sent = sender(ring_out)
    ring = [
        [arrival(ring_in.at[j, 0]), arrival(ring_in.at[j, 1])]
        + [arrival(ring_in.at[j, 2:6])] * 4
        for j in range(CHUNKS)
    ]
    pair_sent = sender(pair_out)
    pairs = [arrival(pair_in.at[j]) for j in range(CHUNKS)]
    quad_sent = sender(quad_out.at[:, 0:3])
    quads = [arrival(quad_in.at[j]) for j in range(CHUNKS)]
    parity, quad = lax.rem(zl, 2), lax.div(zl, 2)

    def chip_sum(j, half, target):
        return part[j, core, half, target] + part_in[j, half, target].astype(F32)

    def ring_send(j, number, value, device):
        ring_out[j, number] = value.astype(BF16)
        remote(
            ring_out.at[j, number], ring_in.at[j, number], ring_sent, ring[j][number][0], device
        ).start()

    def ring_first(j):
        swaps[j][1].wait_recv()
        ring_send(j, 0, chip_sum(j, low, xo), x_peer[1])
        ring_send(j, 1, chip_sum(j, high, xo), x_peer[3])
        ring_send(j, 2, chip_sum(j, high, xp), x_peer[1])
        ring_send(j, 3, chip_sum(j, low, xm), x_peer[3])

    def ring_second(j):
        ring[j][0][1].wait_recv()
        ring_send(j, 4, chip_sum(j, low, xp) + ring_in[j, 0].astype(F32), x_peer[1])
        ring[j][1][1].wait_recv()
        ring_send(j, 5, chip_sum(j, high, xm) + ring_in[j, 1].astype(F32), x_peer[3])

    def line_pair(j):
        ring[j][2][1].wait_recv()
        line_sum[j, low] = (
            chip_sum(j, low, x) + ring_in[j, 3].astype(F32) + ring_in[j, 4].astype(F32)
        )
        line_sum[j, high] = (
            chip_sum(j, high, x) + ring_in[j, 2].astype(F32) + ring_in[j, 5].astype(F32)
        )
        for q in range(4):
            pair_out[j, q] = line_sum[j, 2 * q + 1 - parity].astype(BF16)
        remote(
            pair_out.at[j], pair_in.at[j], pair_sent, pairs[j][0], at(zl_=zl + 1 - 2 * parity)
        ).start()

    def line_quad(j):
        pairs[j][1].wait_recv()
        for q in range(4):
            total = line_sum[j, 2 * q + parity] + pair_in[j, q].astype(F32)
            quad_sum[j, q] = total
            quad_out[j, q] = total.astype(BF16)
        for k in (2, 3, 1):
            other = lax.rem(quad + k, 4)
            remote(
                quad_out.at[j, other],
                quad_in.at[j, k - 1],
                quad_sent,
                quads[j][0],
                at(zl_=2 * other + parity),
            ).start()

    def update(j):
        quads[j][1].wait_recv()
        gradient = quad_sum[j, quad]
        for k in (1, 2, 3):
            gradient = gradient + quad_in[j, k - 1].astype(F32)
        columns = slice(j * CW, (j + 1) * CW)
        one = 0.9 * adam_v[1, 0, :, columns] + 0.1 * gradient
        two = 0.95 * adam_v[2, 0, :, columns] + 0.05 * gradient * gradient
        fresh = adam_v[0, 0, :, columns] - 0.003 * (one / correction_one) / (
            jnp.sqrt(two / correction_two) + 1e-08
        )
        new_one[0, :, columns] = one
        new_two[0, :, columns] = two
        new_master[0, :, columns] = fresh
        weights = fresh.astype(BF16)
        for k in range(CW // 128):
            head = j * (CW // 128) + k
            w_out[head // 4, head % 4] = weights[:, 128 * k : 128 * k + 128]

    lane = lax.broadcasted_iota(jnp.int32, (16, 128), 1)
    diagonal = lane == lax.broadcasted_iota(jnp.int32, (16, 128), 0)
    rows_sent, (rows_sem, rows_here) = sender(rows_z.at[0:7]), arrival(rows_z.at[0:7])
    squares_sent, (squares_sem, squares_here) = (
        sender(squares.at[0:15]),
        arrival(squares.at[0:15]),
    )

    def send_rows():
        own_rows.wait_recv()
        for k in (4, 3, 5, 2, 6, 1, 7):
            other = lax.rem(zl + k, 8)
            remote(
                rows_y.at[:, other], rows_z.at[zl], rows_sent, rows_sem, at(zl_=other)
            ).start()
        total = jnp.zeros((16, 128), F32)
        for q in range(4):
            for k in range(8):
                block = rows_y[q, k].astype(F32)
                total = total + block * block
        column = jnp.sum(total, axis=1, keepdims=True)
        squares[z] = jnp.sum(jnp.where(diagonal, column, 0.0), axis=0, keepdims=True)
        for k in (8, 7, 9, 6, 10, 5, 11, 4, 12, 3, 13, 2, 14, 1, 15):
            remote(squares.at[z], squares.at[z], squares_sent, squares_sem, z_peer(k)).start()
        for q in range(4):
            rows_z[zl, q] = rows_y[q, zl]

    def make_normed():
        gain_load.wait()
        squares_here.wait_recv()
        rows_here.wait_recv()
        for s in range(8):
            both = squares[s] + squares[s + 8]
            column = jnp.sum(jnp.where(diagonal, both, 0.0), axis=1, keepdims=True)
            inverse = lax.rsqrt(column * (1.0 / 8192.0) + 1e-06)
            for q in range(4):
                gain = gain_v[pl.ds((zh * 4 + q) * 8 + zl, 1), :]
                block = rows_z[s, q].astype(F32) * inverse * gain
                normed[16 * s : 16 * s + 16, 128 * q : 128 * q + 128] = block.astype(BF16)

    scale = 1.0 / 128.0**0.5

    def old_scores():
        for copy in score_loads:
            copy.wait()
        q32[...] = jnp.zeros_like(q32)
        for s in range(3):
            for r in range(4):
                q32[32 * r + 8 * s : 32 * r + 8 * s + 8, :] = query_v[s, r].astype(F32)
        sv32[...] = jnp.zeros_like(sv32)
        for s in range(3):
            sv32[4 * s : 4 * s + 4, :] = value_v[s].astype(F32)
        slot = lax.broadcasted_iota(jnp.int32, (32, 512), 1)
        for r in range(4):
            scores = (
                lax.dot_general(
                    q32[32 * r : 32 * r + 32, :].astype(BF16),
                    ck_v[r, 0],
                    (((1,), (1,)), ((), ())),
                    preferred_element_type=F32,
                )
                * scale
            )
            scores = jnp.where(slot < lengths[r], scores, -jnp.inf)
            top = jnp.max(scores, axis=1, keepdims=True)
            weight = jnp.exp(scores - top)
            rows = slice(32 * r, 32 * r + 32)
            old_exp[rows, :] = weight
            old_top[rows, :] = top
            old_sum[rows, :] = jnp.sum(weight, axis=1, keepdims=True)

    shared_sent = [sender(w_all.at[0, 0:31]) for h in range(2)]
    shared = [arrival(w_all.at[0, 0:31]) for h in range(2)]
    keys_sent = sender(key_in.at[0:15, pl.ds(0, 12)])
    keys_sem, keys_here = arrival(key_in.at[0:15, pl.ds(0, 12)])

    def head_columns(h):
        slot = (y * 4 + x) * 2 + core
        for (_, ky, _), device in zip(places, plane):
            remote(
                w_out.at[h, lax.rem(y + ky, 4)],
                w_all.at[h, slot],
                shared_sent[h],
                shared[h][0],
                device,
            ).start()
        w_all[h, slot] = w_out[h, y]

    def send_keys(h):
        shared[h][1].wait_recv()
        key_part[h] = jnp.dot(
            normed[...], w_all[h].reshape(512, 128), preferred_element_type=F32
        ).reshape(8, 16, 128)

        def send(half, line):
            remote(
                key_part.at[half, line, pl.ds(0, 12)],
                key_in.at[z, pl.ds(0, 12)],
                keys_sent,
                keys_sem,
                at(zl_=line, zh_=half),
            ).start()

        if h == 1:
            send(1 - zh, zl)
        for k in (4, 3, 5, 2, 6, 1, 7):
            send(h, lax.rem(zl + k, 8))

    def finish():
        key_in[z] = key_part[zh, zl]
        keys_here.wait_recv()
        total = key_in[0, 0:12]
        for k in range(1, 16):
            total = total + key_in[k, 0:12]
        keys_out[...] = jnp.zeros_like(keys_out)
        keys_out[0:12, :] = total
        keys = keys_out[...].astype(BF16)

        new = (
            lax.dot_general(
                q32[...].astype(BF16), keys, (((1,), (1,)), ((), ())), preferred_element_type=F32
            )
            * scale
        )
        row = lax.broadcasted_iota(jnp.int32, (128, 16), 0)
        column = lax.broadcasted_iota(jnp.int32, (128, 16), 1)
        same_row = (row // 32) == (column % 4)
        earlier = (column // 4) <= ((row % 32) // 8)
        new = jnp.where(same_row & earlier & (column < 12), new, -jnp.inf)
        top = jnp.maximum(old_top[...], jnp.max(new, axis=1, keepdims=True))
        fade = jnp.exp(old_top[...] - top)
        new = jnp.exp(new - top)
        total = old_sum[...] * fade + jnp.sum(new, axis=1, keepdims=True)
        new_probs = (new / total).astype(BF16)
        share = fade / total
        attended = jnp.dot(new_probs, sv32[...].astype(BF16), preferred_element_type=F32)
        for r in range(4):
            rows = slice(32 * r, 32 * r + 32)
            probs = (old_exp[rows, :] * share[rows]).astype(BF16)
            att = attended[rows] + jnp.dot(probs, cv_v[r, 0], preferred_element_type=F32)
            for s in range(3):
                att_out[s, r] = att[8 * s : 8 * s + 8]

    def adam_loads():
        adam_load.wait()

    schedule = (
        (local_term, 0),
        (hop, 1),
        (local_term, 1),
        (hop, 2),
        (ring_first, 0),
        (local_term, 2),
        (hop, 3),
        (ring_first, 1),
        (local_term, 3),
        (hop, 4),
        (ring_second, 0),
        (ring_first, 2),
        (hop, 5),
        (ring_second, 1),
        (line_pair, 0),
        (ring_first, 3),
        (hop, 6),
        (ring_second, 2),
        (line_pair, 1),
        (hop, 7),
        (line_quad, 0),
        (ring_second, 3),
        (line_pair, 2),
        (line_quad, 1),
        (line_pair, 3),
        (line_quad, 2),
        (line_quad, 3),
        (adam_loads,),
        (update, 0),
        (update, 1),
        (head_columns, 0),
        (send_rows,),
        (old_scores,),
        (update, 2),
        (update, 3),
        (head_columns, 1),
        (make_normed,),
        (send_keys, 0),
        (send_keys, 1),
        (finish,),
    )
    for do, *chunk in schedule:
        do(*chunk)

    for copy in sent:
        copy.wait_send()
    assert sems.used == N_SEMS, sems.used


def store(
    master_v, one_v, two_v, keys_v, att_v, step_v, master, one, two, keys, decoded, keys_b, dec_b, sems
):
    copies = []

    def start(src, dst):
        copies.append(pltpu.make_async_copy(src, dst, sems.at[len(copies)]))
        copies[-1].start()

    start(master_v, master)
    start(one_v, one)
    start(two_v, two)
    for s in range(3):
        keys_b[s] = keys_v[4 * s : 4 * s + 4, :].astype(BF16)
    start(keys_b, keys)
    for s in range(3):
        for g in range(8):
            columns = slice(128 * g, 128 * g + 128)
            dec_b[s, :, columns] = (
                step_v[s, :, columns].astype(F32) + att_v[s, :, g, :]
            ).astype(BF16)
    start(dec_b, decoded)
    for copy in copies:
        copy.wait()


def body(
    train_inputs,
    key_cotangent,
    master,
    moment_one,
    moment_two,
    step_inputs,
    decode_queries,
    step_values,
    cache_keys,
    cache_values,
    cache_lengths,
    norm_gain,
):
    hbm = pl.BlockSpec(memory_space=pltpu.HBM)
    vmem = pl.BlockSpec(memory_space=pltpu.VMEM)
    owned = jax.ShapeDtypeStruct(master.shape, F32)
    owned_v = pltpu.VMEM(master.shape, F32)
    results = pl.pallas_call(
        kernel,
        out_shape=(
            owned_v,
            owned_v,
            owned_v,
            pltpu.VMEM((16, 128), F32),
            pltpu.VMEM((3, 4, 8, 128), F32),
        ),
        in_specs=[hbm] * 12,
        out_specs=(vmem,) * 5,
        scratch_shapes=[
            pltpu.VMEM((1024, 1024), BF16),
            pltpu.VMEM((1024, 1024), BF16),
            pltpu.VMEM((3, 1, 16, 1024), F32),
            pltpu.VMEM((3, 4, 1024), BF16),
            pltpu.VMEM((3, 4, 8, 128), BF16),
            pltpu.VMEM((3, 4, 128), BF16),
            pltpu.VMEM((4, 1, 512, 128), BF16),
            pltpu.VMEM((4, 1, 512, 128), BF16),
            pltpu.VMEM((64, 128), F32),
            pltpu.SMEM((4,), jnp.int32),
            pltpu.VMEM((CHUNKS, 2, 8, 4, 16, CW), F32),
            pltpu.VMEM((CHUNKS, 8, 4, 16, CW), BF16),
            pltpu.VMEM((CHUNKS, 8, 4, 16, CW), BF16),
            pltpu.VMEM((CHUNKS, 6, 4, 16, CW), BF16),
            pltpu.VMEM((CHUNKS, 6, 4, 16, CW), BF16),
            pltpu.VMEM((CHUNKS, 8, 16, CW), F32),
            pltpu.VMEM((CHUNKS, 4, 16, CW), BF16),
            pltpu.VMEM((CHUNKS, 4, 16, CW), BF16),
            pltpu.VMEM((CHUNKS, 4, 16, CW), F32),
            pltpu.VMEM((CHUNKS, 4, 16, CW), BF16),
            pltpu.VMEM((CHUNKS, 3, 16, CW), BF16),
            pltpu.VMEM((16, 1024), F32),
            pltpu.VMEM((4, 8, 16, 128), BF16),
            pltpu.VMEM((8, 4, 16, 128), BF16),
            pltpu.VMEM((16, 1, 128), F32),
            pltpu.VMEM((128, 512), BF16),
            pltpu.VMEM((2, 4, 16, 128), BF16),
            pltpu.VMEM((2, 32, 16, 128), BF16),
            pltpu.VMEM((2, 8, 16, 128), F32),
            pltpu.VMEM((16, 16, 128), F32),
            pltpu.VMEM((128, 128), F32),
            pltpu.VMEM((128, 512), F32),
            pltpu.VMEM((128, 1), F32),
            pltpu.VMEM((128, 1), F32),
            pltpu.VMEM((16, 128), F32),
            pltpu.SemaphoreType.DMA((N_SEMS,)),
            pltpu.SemaphoreType.REGULAR((7,)),
        ],
        compiler_params=pltpu.CompilerParams(
            collective_id=0, has_side_effects=True, vmem_limit_bytes=40 << 20
        ),
        name="adam_decode",
    )(
        *(
            pltpu.with_memory_space_constraint(array, pltpu.HBM)
            for array in (
                train_inputs,
                key_cotangent,
                master,
                moment_one,
                moment_two,
                step_inputs,
                decode_queries,
                step_values.reshape(3, 4, 128),
                cache_keys,
                cache_values,
                cache_lengths,
                norm_gain.reshape(64, 128),
            )
        ),
    )
    new_master, new_one, new_two, new_keys, decoded = pl.pallas_call(
        store,
        out_shape=(
            owned,
            owned,
            owned,
            jax.ShapeDtypeStruct((3, 4, 128), BF16),
            jax.ShapeDtypeStruct(step_inputs.shape, BF16),
        ),
        in_specs=[vmem] * 6,
        out_specs=(hbm,) * 5,
        scratch_shapes=[
            pltpu.VMEM((3, 4, 128), BF16),
            pltpu.VMEM((3, 4, 1024), BF16),
            pltpu.SemaphoreType.DMA((5,)),
        ],
        compiler_params=pltpu.CompilerParams(vmem_limit_bytes=40 << 20),
        name="store_results",
    )(*results, step_inputs)
    return new_master, new_one, new_two, new_keys.reshape(step_values.shape), decoded


def solution(mesh):
    return jax.shard_map(
        body,
        mesh=mesh,
        in_specs=(
            P("fsdp", "tp"),
            P("fsdp", None),
            P("tp", "fsdp", None),
            P("tp", "fsdp", None),
            P("tp", "fsdp", None),
            P(None, "fsdp", "tp"),
            P(None, "fsdp", "tp", None),
            P(None, "fsdp", "tp", None),
            P("fsdp", "tp", None, None),
            P("fsdp", "tp", None, None),
            P("fsdp"),
            P(),
        ),
        out_specs=(
            P("tp", "fsdp", None),
            P("tp", "fsdp", None),
            P("tp", "fsdp", None),
            P(None, "fsdp", "tp", None),
            P(None, "fsdp", "tp"),
        ),
        check_vma=False,
    )
```

```python
import functools

import jax
import jax.numpy as jnp
from jax import lax
from jax.experimental import pallas as pl
from jax.experimental.pallas import tpu as pltpu
from jax.sharding import PartitionSpec as P

MESH = pl.DeviceIdType.MESH
correction_one = 1.0 - 0.9**4
correction_two = 1.0 - 0.95**4

CHUNKS = 4
CW = 1024 // CHUNKS
F32 = jnp.float32
BF16 = jnp.bfloat16


class Sems:
    def __init__(self, sems):
        self.sems, self.used = sems, 0

    def new(self):
        self.used += 1
        return self.sems.at[self.used - 1]


def remote(src, dst, send_sem, recv_sem, device):
    return pltpu.make_async_remote_copy(
        src_ref=src,
        dst_ref=dst,
        send_sem=send_sem,
        recv_sem=recv_sem,
        device_id=device,
        device_id_type=MESH,
    )


N_SEMS = 25 + 7 * CHUNKS


def kernel(
    x_hbm,
    c_hbm,
    master_hbm,
    one_hbm,
    two_hbm,
    step_hbm,
    query_hbm,
    value_hbm,
    ck_hbm,
    cv_hbm,
    lengths_hbm,
    gain_hbm,
    new_master,
    new_one,
    new_two,
    keys_out,
    att_out,
    x_v,
    c_v,
    adam_v,
    step_v,
    query_v,
    value_v,
    ck_v,
    cv_v,
    gain_v,
    lengths,
    part,
    part_out,
    part_in,
    ring_out,
    ring_in,
    line_sum,
    pair_out,
    pair_in,
    quad_sum,
    quad_out,
    quad_in,
    rows32,
    rows_y,
    rows_z,
    squares,
    normed,
    w_out,
    w_all,
    key_part,
    key_in,
    q32,
    old_exp,
    old_top,
    old_sum,
    sv32,
    copy_sems,
    far_sems,
):
    f, t = lax.axis_index("fsdp"), lax.axis_index("tp")
    core = lax.rem(f, 2)
    x = lax.rem(lax.div(f, 2), 4)
    zl = lax.div(f, 8)
    y = lax.rem(t, 4)
    zh = lax.div(t, 4)
    z = zh * 8 + zl

    def fsdp(zl_, x_, core_):
        return (zl_ * 4 + x_) * 2 + core_

    def at(zl_=zl, x_=x, core_=core, zh_=zh, y_=y):
        return {"fsdp": fsdp(zl_, x_, core_), "tp": zh_ * 4 + y_}

    sibling = at(core_=1 - core)
    x_peer = [None] + [at(x_=lax.rem(x + k, 4)) for k in (1, 2, 3)]
    y_peer = [None] + [at(y_=lax.rem(y + k, 4)) for k in (1, 2, 3)]

    def z_of(k):
        return lax.rem(z + k, 16)

    def z_peer(k):
        other = z_of(k)
        return at(zl_=lax.rem(other, 8), zh_=lax.div(other, 8))

    sems = Sems(copy_sems)

    barrier = pltpu.get_barrier_semaphore()
    places = [
        (kx, ky, kc) for kx in (2, 1, 3, 0) for ky in (2, 1, 3, 0) for kc in (0, 1)
    ]
    places.remove((0, 0, 0))
    places.sort(key=lambda place: -(min(place[0], 4 - place[0]) + min(place[1], 4 - place[1])))
    plane = [
        at(x_=lax.rem(x + kx, 4), y_=lax.rem(y + ky, 4), core_=1 - core if kc else core)
        for kx, ky, kc in places
    ]
    partners = plane + [z_peer(1), z_peer(15)]
    for partner in partners:
        pl.semaphore_signal(barrier, inc=1, device_id=partner, device_id_type=MESH)

    def load(pairs, whole=None):
        sem = sems.new()
        for src, dst in pairs:
            pltpu.make_async_copy(src, dst, sem).start()
        return pltpu.make_async_copy(*(whole or pairs[0]), sem)

    step_load = load([(step_hbm, step_v)])
    x_load = load([(x_hbm, x_v)])
    c_loads = []
    for j in range(CHUNKS):
        columns = slice(j * CW, (j + 1) * CW)
        c_loads.append(load([(c_hbm.at[:, columns], c_v.at[:, columns])]))
    score_loads = [
        load([pair])
        for pair in (
            (query_hbm, query_v),
            (ck_hbm, ck_v),
            (cv_hbm, cv_v),
            (value_hbm, value_v),
            (lengths_hbm, lengths),
        )
    ]
    gain_load = load([(gain_hbm, gain_v)])
    adam_load = load(
        [(ref, adam_v.at[k]) for k, ref in enumerate((master_hbm, one_hbm, two_hbm))],
        (adam_v, adam_v),
    )

    step_load.wait()
    rows32[...] = jnp.zeros_like(rows32)
    for s in range(3):
        rows32[4 * s : 4 * s + 4, :] = step_v[s].astype(F32)
    for k in range(8):
        rows_y[y, k] = rows32[:, 128 * k : 128 * k + 128].astype(BF16)

    pl.semaphore_wait(barrier, len(partners))
    sent = []

    def sender(whole):
        sem = sems.new()
        sent.append(remote(whole, whole, sem, sem, sibling))
        return sem

    def arrival(whole):
        sem = sems.new()
        return sem, remote(whole, whole, sem, sem, sibling)

    def hop(d):
        if d > 0:
            pl.semaphore_wait(far_sems.at[d - 1], 2)
        if d < 7:
            for partner in (z_peer(1), z_peer(15)):
                pl.semaphore_signal(
                    far_sems.at[d], inc=1, device_id=partner, device_id_type=MESH
                )

    hop(0)
    own_sent, (own_sem, own_rows) = sender(rows_y.at[0:3]), arrival(rows_y.at[0:3])
    for k in (2, 1, 3):
        remote(rows_y.at[y], rows_y.at[y], own_sent, own_sem, y_peer[k]).start()

    swap_sent = sender(part_out)
    swaps = [arrival(part_in.at[j]) for j in range(CHUNKS)]

    def local_term(j):
        if j == 0:
            x_load.wait()
        c_loads[j].wait()
        term = lax.dot_general(
            x_v[...],
            c_v[:, j * CW : (j + 1) * CW],
            (((0,), (0,)), ((), ())),
            preferred_element_type=F32,
        ).reshape(8, 4, 2, 16, CW)
        part[j, 0] = term[:, :, 0]
        part[j, 1] = term[:, :, 1]
        part_out[j] = part[j, 1 - core].astype(BF16)
        remote(part_out.at[j], part_in.at[j], swap_sent, swaps[j][0], sibling).start()

    xp, xo, xm = (lax.rem(x + k, 4) for k in (1, 2, 3))
    low, high = slice(0, 4), slice(4, 8)
    ring_sent = sender(ring_out)
    ring = [
        [arrival(ring_in.at[j, 0]), arrival(ring_in.at[j, 1])]
        + [arrival(ring_in.at[j, 2:6])] * 4
        for j in range(CHUNKS)
    ]
    pair_sent = sender(pair_out)
    pairs = [arrival(pair_in.at[j]) for j in range(CHUNKS)]
    quad_sent = sender(quad_out.at[:, 0:3])
    quads = [arrival(quad_in.at[j]) for j in range(CHUNKS)]
    parity, quad = lax.rem(zl, 2), lax.div(zl, 2)

    def chip_sum(j, half, target):
        return part[j, core, half, target] + part_in[j, half, target].astype(F32)

    def ring_send(j, number, value, device):
        ring_out[j, number] = value.astype(BF16)
        remote(
            ring_out.at[j, number], ring_in.at[j, number], ring_sent, ring[j][number][0], device
        ).start()

    def ring_first(j):
        swaps[j][1].wait_recv()
        ring_send(j, 0, chip_sum(j, low, xo), x_peer[1])
        ring_send(j, 1, chip_sum(j, high, xo), x_peer[3])
        ring_send(j, 2, chip_sum(j, high, xp), x_peer[1])
        ring_send(j, 3, chip_sum(j, low, xm), x_peer[3])

    def ring_second(j):
        ring[j][0][1].wait_recv()
        ring_send(j, 4, chip_sum(j, low, xp) + ring_in[j, 0].astype(F32), x_peer[1])
        ring[j][1][1].wait_recv()
        ring_send(j, 5, chip_sum(j, high, xm) + ring_in[j, 1].astype(F32), x_peer[3])

    def line_pair(j):
        ring[j][2][1].wait_recv()
        line_sum[j, low] = (
            chip_sum(j, low, x) + ring_in[j, 3].astype(F32) + ring_in[j, 4].astype(F32)
        )
        line_sum[j, high] = (
            chip_sum(j, high, x) + ring_in[j, 2].astype(F32) + ring_in[j, 5].astype(F32)
        )
        for q in range(4):
            pair_out[j, q] = line_sum[j, 2 * q + 1 - parity].astype(BF16)
        remote(
            pair_out.at[j], pair_in.at[j], pair_sent, pairs[j][0], at(zl_=zl + 1 - 2 * parity)
        ).start()

    def line_quad(j):
        pairs[j][1].wait_recv()
        for q in range(4):
            total = line_sum[j, 2 * q + parity] + pair_in[j, q].astype(F32)
            quad_sum[j, q] = total
            quad_out[j, q] = total.astype(BF16)
        for k in (2, 3, 1):
            other = lax.rem(quad + k, 4)
            remote(
                quad_out.at[j, other],
                quad_in.at[j, k - 1],
                quad_sent,
                quads[j][0],
                at(zl_=2 * other + parity),
            ).start()

    def update(j):
        quads[j][1].wait_recv()
        gradient = quad_sum[j, quad]
        for k in (1, 2, 3):
            gradient = gradient + quad_in[j, k - 1].astype(F32)
        columns = slice(j * CW, (j + 1) * CW)
        one = 0.9 * adam_v[1, 0, :, columns] + 0.1 * gradient
        two = 0.95 * adam_v[2, 0, :, columns] + 0.05 * gradient * gradient
        fresh = adam_v[0, 0, :, columns] - 0.003 * (one / correction_one) / (
            jnp.sqrt(two / correction_two) + 1e-08
        )
        new_one[0, :, columns] = one
        new_two[0, :, columns] = two
        new_master[0, :, columns] = fresh
        weights = fresh.astype(BF16)
        for k in range(CW // 128):
            head = j * (CW // 128) + k
            w_out[head // 4, head % 4] = weights[:, 128 * k : 128 * k + 128]

    lane = lax.broadcasted_iota(jnp.int32, (16, 128), 1)
    diagonal = lane == lax.broadcasted_iota(jnp.int32, (16, 128), 0)
    rows_sent, (rows_sem, rows_here) = sender(rows_z.at[0:7]), arrival(rows_z.at[0:7])
    squares_sent, (squares_sem, squares_here) = (
        sender(squares.at[0:15]),
        arrival(squares.at[0:15]),
    )

    def send_rows():
        own_rows.wait_recv()
        for k in (4, 3, 5, 2, 6, 1, 7):
            other = lax.rem(zl + k, 8)
            remote(
                rows_y.at[:, other], rows_z.at[zl], rows_sent, rows_sem, at(zl_=other)
            ).start()
        total = jnp.zeros((16, 128), F32)
        for q in range(4):
            for k in range(8):
                block = rows_y[q, k].astype(F32)
                total = total + block * block
        column = jnp.sum(total, axis=1, keepdims=True)
        squares[z] = jnp.sum(jnp.where(diagonal, column, 0.0), axis=0, keepdims=True)
        for k in (8, 7, 9, 6, 10, 5, 11, 4, 12, 3, 13, 2, 14, 1, 15):
            remote(squares.at[z], squares.at[z], squares_sent, squares_sem, z_peer(k)).start()
        for q in range(4):
            rows_z[zl, q] = rows_y[q, zl]

    def make_normed():
        gain_load.wait()
        squares_here.wait_recv()
        rows_here.wait_recv()
        for s in range(8):
            both = squares[s] + squares[s + 8]
            column = jnp.sum(jnp.where(diagonal, both, 0.0), axis=1, keepdims=True)
            inverse = lax.rsqrt(column * (1.0 / 8192.0) + 1e-06)
            for q in range(4):
                gain = gain_v[pl.ds((zh * 4 + q) * 8 + zl, 1), :]
                block = rows_z[s, q].astype(F32) * inverse * gain
                normed[16 * s : 16 * s + 16, 128 * q : 128 * q + 128] = block.astype(BF16)

    scale = 1.0 / 128.0**0.5

    def old_scores():
        for copy in score_loads:
            copy.wait()
        q32[...] = jnp.zeros_like(q32)
        for s in range(3):
            for r in range(4):
                q32[32 * r + 8 * s : 32 * r + 8 * s + 8, :] = query_v[s, r].astype(F32)
        sv32[...] = jnp.zeros_like(sv32)
        for s in range(3):
            sv32[4 * s : 4 * s + 4, :] = value_v[s].astype(F32)
        slot = lax.broadcasted_iota(jnp.int32, (32, 512), 1)
        for r in range(4):
            scores = (
                lax.dot_general(
                    q32[32 * r : 32 * r + 32, :].astype(BF16),
                    ck_v[r, 0],
                    (((1,), (1,)), ((), ())),
                    preferred_element_type=F32,
                )
                * scale
            )
            scores = jnp.where(slot < lengths[r], scores, -jnp.inf)
            top = jnp.max(scores, axis=1, keepdims=True)
            weight = jnp.exp(scores - top)
            rows = slice(32 * r, 32 * r + 32)
            old_exp[rows, :] = weight
            old_top[rows, :] = top
            old_sum[rows, :] = jnp.sum(weight, axis=1, keepdims=True)

    shared_sent = [sender(w_all.at[0, 0:31]) for h in range(2)]
    shared = [arrival(w_all.at[0, 0:31]) for h in range(2)]
    keys_sent = sender(key_in.at[0:15, pl.ds(0, 12)])
    keys_sem, keys_here = arrival(key_in.at[0:15, pl.ds(0, 12)])

    def head_columns(h):
        slot = (y * 4 + x) * 2 + core
        for (_, ky, _), device in zip(places, plane):
            remote(
                w_out.at[h, lax.rem(y + ky, 4)],
                w_all.at[h, slot],
                shared_sent[h],
                shared[h][0],
                device,
            ).start()
        w_all[h, slot] = w_out[h, y]

    def send_keys(h):
        shared[h][1].wait_recv()
        key_part[h] = jnp.dot(
            normed[...], w_all[h].reshape(512, 128), preferred_element_type=F32
        ).reshape(8, 16, 128)

        def send(half, line):
            remote(
                key_part.at[half, line, pl.ds(0, 12)],
                key_in.at[z, pl.ds(0, 12)],
                keys_sent,
                keys_sem,
                at(zl_=line, zh_=half),
            ).start()

        if h == 1:
            send(1 - zh, zl)
        for k in (4, 3, 5, 2, 6, 1, 7):
            send(h, lax.rem(zl + k, 8))

    def finish():
        key_in[z] = key_part[zh, zl]
        keys_here.wait_recv()
        total = key_in[0, 0:12]
        for k in range(1, 16):
            total = total + key_in[k, 0:12]
        keys_out[...] = jnp.zeros_like(keys_out)
        keys_out[0:12, :] = total
        keys = keys_out[...].astype(BF16)

        new = (
            lax.dot_general(
                q32[...].astype(BF16), keys, (((1,), (1,)), ((), ())), preferred_element_type=F32
            )
            * scale
        )
        row = lax.broadcasted_iota(jnp.int32, (128, 16), 0)
        column = lax.broadcasted_iota(jnp.int32, (128, 16), 1)
        same_row = (row // 32) == (column % 4)
        earlier = (column // 4) <= ((row % 32) // 8)
        new = jnp.where(same_row & earlier & (column < 12), new, -jnp.inf)
        top = jnp.maximum(old_top[...], jnp.max(new, axis=1, keepdims=True))
        fade = jnp.exp(old_top[...] - top)
        new = jnp.exp(new - top)
        total = old_sum[...] * fade + jnp.sum(new, axis=1, keepdims=True)
        new_probs = (new / total).astype(BF16)
        share = fade / total
        attended = jnp.dot(new_probs, sv32[...].astype(BF16), preferred_element_type=F32)
        for r in range(4):
            rows = slice(32 * r, 32 * r + 32)
            probs = (old_exp[rows, :] * share[rows]).astype(BF16)
            att = attended[rows] + jnp.dot(probs, cv_v[r, 0], preferred_element_type=F32)
            for s in range(3):
                att_out[s, r] = att[8 * s : 8 * s + 8]

    def adam_loads():
        adam_load.wait()

    schedule = (
        (local_term, 0),
        (hop, 1),
        (local_term, 1),
        (hop, 2),
        (ring_first, 0),
        (local_term, 2),
        (hop, 3),
        (ring_first, 1),
        (local_term, 3),
        (hop, 4),
        (ring_second, 0),
        (ring_first, 2),
        (hop, 5),
        (ring_second, 1),
        (line_pair, 0),
        (ring_first, 3),
        (hop, 6),
        (ring_second, 2),
        (line_pair, 1),
        (hop, 7),
        (line_quad, 0),
        (ring_second, 3),
        (line_pair, 2),
        (line_pair, 3),
        (line_quad, 1),
        (line_quad, 2),
        (line_quad, 3),
        (adam_loads,),
        (update, 0),
        (update, 1),
        (head_columns, 0),
        (send_rows,),
        (old_scores,),
        (update, 2),
        (update, 3),
        (head_columns, 1),
        (make_normed,),
        (send_keys, 0),
        (send_keys, 1),
        (finish,),
    )
    for do, *chunk in schedule:
        do(*chunk)

    for copy in sent:
        copy.wait_send()
    assert sems.used == N_SEMS, sems.used


def store(
    master_v, one_v, two_v, keys_v, att_v, step_v, master, one, two, keys, decoded, keys_b, dec_b, sems
):
    copies = []

    def start(src, dst):
        copies.append(pltpu.make_async_copy(src, dst, sems.at[len(copies)]))
        copies[-1].start()

    start(master_v, master)
    start(one_v, one)
    start(two_v, two)
    for s in range(3):
        keys_b[s] = keys_v[4 * s : 4 * s + 4, :].astype(BF16)
    start(keys_b, keys)
    for s in range(3):
        for g in range(8):
            columns = slice(128 * g, 128 * g + 128)
            dec_b[s, :, columns] = (
                step_v[s, :, columns].astype(F32) + att_v[s, :, g, :]
            ).astype(BF16)
    start(dec_b, decoded)
    for copy in copies:
        copy.wait()


def body(
    train_inputs,
    key_cotangent,
    master,
    moment_one,
    moment_two,
    step_inputs,
    decode_queries,
    step_values,
    cache_keys,
    cache_values,
    cache_lengths,
    norm_gain,
):
    hbm = pl.BlockSpec(memory_space=pltpu.HBM)
    vmem = pl.BlockSpec(memory_space=pltpu.VMEM)
    owned = jax.ShapeDtypeStruct(master.shape, F32)
    owned_v = pltpu.VMEM(master.shape, F32)
    results = pl.pallas_call(
        kernel,
        out_shape=(
            owned_v,
            owned_v,
            owned_v,
            pltpu.VMEM((16, 128), F32),
            pltpu.VMEM((3, 4, 8, 128), F32),
        ),
        in_specs=[hbm] * 12,
        out_specs=(vmem,) * 5,
        scratch_shapes=[
            pltpu.VMEM((1024, 1024), BF16),
            pltpu.VMEM((1024, 1024), BF16),
            pltpu.VMEM((3, 1, 16, 1024), F32),
            pltpu.VMEM((3, 4, 1024), BF16),
            pltpu.VMEM((3, 4, 8, 128), BF16),
            pltpu.VMEM((3, 4, 128), BF16),
            pltpu.VMEM((4, 1, 512, 128), BF16),
            pltpu.VMEM((4, 1, 512, 128), BF16),
            pltpu.VMEM((64, 128), F32),
            pltpu.SMEM((4,), jnp.int32),
            pltpu.VMEM((CHUNKS, 2, 8, 4, 16, CW), F32),
            pltpu.VMEM((CHUNKS, 8, 4, 16, CW), BF16),
            pltpu.VMEM((CHUNKS, 8, 4, 16, CW), BF16),
            pltpu.VMEM((CHUNKS, 6, 4, 16, CW), BF16),
            pltpu.VMEM((CHUNKS, 6, 4, 16, CW), BF16),
            pltpu.VMEM((CHUNKS, 8, 16, CW), F32),
            pltpu.VMEM((CHUNKS, 4, 16, CW), BF16),
            pltpu.VMEM((CHUNKS, 4, 16, CW), BF16),
            pltpu.VMEM((CHUNKS, 4, 16, CW), F32),
            pltpu.VMEM((CHUNKS, 4, 16, CW), BF16),
            pltpu.VMEM((CHUNKS, 3, 16, CW), BF16),
            pltpu.VMEM((16, 1024), F32),
            pltpu.VMEM((4, 8, 16, 128), BF16),
            pltpu.VMEM((8, 4, 16, 128), BF16),
            pltpu.VMEM((16, 1, 128), F32),
            pltpu.VMEM((128, 512), BF16),
            pltpu.VMEM((2, 4, 16, 128), BF16),
            pltpu.VMEM((2, 32, 16, 128), BF16),
            pltpu.VMEM((2, 8, 16, 128), F32),
            pltpu.VMEM((16, 16, 128), F32),
            pltpu.VMEM((128, 128), F32),
            pltpu.VMEM((128, 512), F32),
            pltpu.VMEM((128, 1), F32),
            pltpu.VMEM((128, 1), F32),
            pltpu.VMEM((16, 128), F32),
            pltpu.SemaphoreType.DMA((N_SEMS,)),
            pltpu.SemaphoreType.REGULAR((7,)),
        ],
        compiler_params=pltpu.CompilerParams(
            collective_id=0, has_side_effects=True, vmem_limit_bytes=40 << 20
        ),
        name="adam_decode",
    )(
        *(
            pltpu.with_memory_space_constraint(array, pltpu.HBM)
            for array in (
                train_inputs,
                key_cotangent,
                master,
                moment_one,
                moment_two,
                step_inputs,
                decode_queries,
                step_values.reshape(3, 4, 128),
                cache_keys,
                cache_values,
                cache_lengths,
                norm_gain.reshape(64, 128),
            )
        ),
    )
    new_master, new_one, new_two, new_keys, decoded = pl.pallas_call(
        store,
        out_shape=(
            owned,
            owned,
            owned,
            jax.ShapeDtypeStruct((3, 4, 128), BF16),
            jax.ShapeDtypeStruct(step_inputs.shape, BF16),
        ),
        in_specs=[vmem] * 6,
        out_specs=(hbm,) * 5,
        scratch_shapes=[
            pltpu.VMEM((3, 4, 128), BF16),
            pltpu.VMEM((3, 4, 1024), BF16),
            pltpu.SemaphoreType.DMA((5,)),
        ],
        compiler_params=pltpu.CompilerParams(vmem_limit_bytes=40 << 20),
        name="store_results",
    )(*results, step_inputs)
    return new_master, new_one, new_two, new_keys.reshape(step_values.shape), decoded


def solution(mesh):
    return jax.shard_map(
        body,
        mesh=mesh,
        in_specs=(
            P("fsdp", "tp"),
            P("fsdp", None),
            P("tp", "fsdp", None),
            P("tp", "fsdp", None),
            P("tp", "fsdp", None),
            P(None, "fsdp", "tp"),
            P(None, "fsdp", "tp", None),
            P(None, "fsdp", "tp", None),
            P("fsdp", "tp", None, None),
            P("fsdp", "tp", None, None),
            P("fsdp"),
            P(),
        ),
        out_specs=(
            P("tp", "fsdp", None),
            P("tp", "fsdp", None),
            P("tp", "fsdp", None),
            P(None, "fsdp", "tp", None),
            P(None, "fsdp", "tp"),
        ),
        check_vma=False,
    )
```
